1024 devices in a mesh: group: 16 (over z), member: 16 (over y, core), dp: 4 (over x).
Axes of the slice: x: 4, y: 8, z: 16, core: 2. Of those that a mesh axis runs over, the one named last changes fastest.
Arguments:
- out_grad: bfloat16 [24576, 2560], P(('dp', 'group', 'member')), parts along dimension 0, may hold values from -6 to 6
- groups: int32 [24576, 3], P(('dp', 'group', 'member')), parts along dimension 0, may hold values from 0 to 15, all different within a row; in each aligned block of 24 rows (0 to 23, 24 to 47, ...) at most 9 rows name the same one
- picks: int32 [24576, 6], P(('dp', 'group', 'member')), parts along dimension 0, may hold values from 0 to 23, all different within a row
- gates: bfloat16 [24576, 6], P(('dp', 'group', 'member')), parts along dimension 0, may hold values from 0.099609375 to 1
- w_gate: bfloat16 [16, 16, 2560, 384], P('group', 'member'), may hold values from -0.125 to 0.125
- w_up: bfloat16 [16, 16, 2560, 384], P('group', 'member'), may hold values from -0.125 to 0.125
- w_down: bfloat16 [16, 16, 384, 2560], P('group', 'member'), may hold values from -0.21875 to 0.21875
- saved: bfloat16 [16, 16, 1152, 2560], P('group', 'member', 'dp'), parts along dimension 2, may hold values from -6 to 6
Outputs:
- input_grad: bfloat16 [24576, 2560], P(('dp', 'group', 'member')), parts along dimension 0
The draws below stay inside these ranges and needn't reach their ends.
There are 4 independent parts, one for each index of `dp`. The reference program is written for one: setup_inputs(seed, part) draws one part's arguments, and reference() takes and returns one part's arrays. A program takes and returns all parts, laid end to end along the dimension named above; an argument that names none is the same for every part. Nothing has to cross between parts.
Inputs may be any that keep to these rules, and one draw needn't show every extreme that they name: Each row names three different groups; in each aligned block of 24 rows (the rows of one device) no group is named by more than 9 rows, a bound that some block reaches. `picks`: each row names 6 different positions.
All inputs are finite; a program needn't handle non-finite values.
Results may differ from the reference program's by a relative error of at most 0.015.
Values may be sent and summed in bfloat16 or wider, within the bound.
No kernel may reach another device: no remote copies, remote signals or barrier semaphores. Data moves between devices by JAX's collectives and lax.ppermute only.
A program may use at most 32 MiB of HBM per device.

```python
import math
import jax
import jax.numpy as jnp
import numpy as np
from jax import lax

D = 2560
FF = 768
TOP = 6
GROUP_TOP = 3
TOK_DEV = 24
FF_DEV = 384
EXP_GROUP = 8
EXPERTS = 128
GROUP_CAP = 9
MEMBER_CAP = 18
SLOTS = 288
TOKENS = 6144
N_GROUP = 16
N_MEMBER = 16


def block_levels(rng, extent, shards, smallest, largest):
    def one(position, blocks):
        heights = jax.random.uniform(jax.random.fold_in(jax.random.fold_in(rng, 6), position), (blocks,), jnp.float32, smallest / len(shards), largest / len(shards))
        return jnp.repeat(jnp.exp(heights), extent[position] // blocks).reshape((-1,) + (1,) * (len(extent) - position - 1))

    factor_of = one(*shards[0])
    for cut in shards[1:]:
        factor_of = factor_of * one(*cut)
    return factor_of


def picks_of(rng, rows, number_of, top, lift):
    sequence = jax.random.permutation(jax.random.fold_in(rng, 1), number_of)
    favour = sequence
    for power in range(3):
        favour = favour * favour // number_of
    favour = favour * lift // number_of
    lots = jax.random.randint(jax.random.fold_in(rng, 2), (rows, number_of), 0, 4096) + favour
    holders = jax.random.permutation(jax.random.fold_in(rng, 3), rows)[jnp.arange(number_of) % rows]
    lots = jnp.where(jnp.arange(rows)[:, None] == holders[None, :], 1 << 14, lots)
    score = lots * number_of + jnp.arange(number_of)
    return lax.top_k(score.astype(jnp.int32), top)[1].astype(jnp.int32)


def routed_block(own_key, own, number, rows, amount, top, most, slope):
    order = jax.random.permutation(own_key, amount)
    crowded, usual = shares(amount, rows * top, most, slope, True), shares(amount, rows * top, most, slope, False)
    places = jnp.arange(amount)

    def named(sizes, turn):
        used = int((sizes > 0).sum())
        fixed = max(1, used // 4)
        shifted = fixed + (places - fixed + turn * (used - fixed)) % max(1, amount - fixed)
        return jnp.zeros((amount,), jnp.int32).at[order[jnp.where(places < fixed, places, shifted)]].set(jnp.asarray(sizes, jnp.int32))

    sizes = jnp.where(number % 4 == 0, named(crowded, number // 4), named(usual, number - number // 4 - 1))
    mixed = jax.random.permutation(jax.random.fold_in(own, 3), amount)
    donor, taker = mixed[0:amount // 2 * 2:2], mixed[1:amount // 2 * 2:2]
    slack = jnp.minimum(sizes[donor] - 1, most - sizes[taker]) // 2
    slack = jnp.where((donor == order[0]) | (taker == order[0]) | (sizes[taker] == 0), 0, jnp.maximum(slack, 0))
    shifted = jax.random.randint(jax.random.fold_in(own, 4), (amount // 2,), 0, 1 << 20) % (slack + 1)
    sizes = sizes.at[donor].add(-shifted).at[taker].add(shifted)
    labels = jnp.searchsorted(jnp.cumsum(sizes), jnp.arange(rows * top), side="right").astype(jnp.int32)
    listing = labels.reshape(top, rows).T
    listing = listing[jax.random.permutation(jax.random.fold_in(own, 1), rows)]
    turn = jax.random.randint(jax.random.fold_in(own, 2), (rows, 1), 0, top)
    return jnp.take_along_axis(listing, (jnp.arange(top)[None, :] + turn) % top, axis=1)


def shares(count, total, most, lean, full):
    loads = [(1 << 20) // math.isqrt(standing ** lean) + 1 for standing in range(1, count + 1)]
    largest = most if full else min(most, max(-(-total // count), total * loads[0] // sum(loads)))
    least = 1 if total - largest >= count - 1 else 0
    counts, surplus = [largest] + [least] * (count - 1), total - largest - least * (count - 1)
    while surplus > 0:
        movable = [i for i in range(1, count) if counts[i] < largest] or [i for i in range(1, count) if counts[i] < most]
        whole, left = sum([loads[i] for i in movable]), surplus
        for i in movable:
            extra = min(most - counts[i], max(1, left * loads[i] // whole), surplus)
            counts[i] = counts[i] + extra
            surplus = surplus - extra
    return np.array(counts)


def gaussian(own_key, extent, width, bound, shards=(), kind=jnp.bfloat16):
    entries = jax.random.normal(own_key, extent, jnp.float32) * width
    if len(shards) > 0:
        entries = block_levels(own_key, extent, shards, -0.22, 0.18) * entries
    return jnp.clip(entries, min=-bound, max=bound).astype(kind)


def setup_inputs(seed: int = 0, part: int = 0) -> dict:
    splits = jax.random.split(jax.random.key(seed), 9)
    part_keys = jax.random.split(jax.random.fold_in(splits[8], part), 9)
    out_grad = gaussian(part_keys[0], (TOKENS, D), 1.0, 6.0, ((0, 256),))
    groups_keys = jax.random.split(jax.random.fold_in(part_keys[1], 1), TOKENS // TOK_DEV)
    groups_turns = jax.random.permutation(jax.random.fold_in(part_keys[1], 3), TOKENS // TOK_DEV)
    groups = jax.vmap(lambda own, number: routed_block(jax.random.fold_in(part_keys[1], 2), own, number, TOK_DEV, N_GROUP, GROUP_TOP, GROUP_CAP, 2))(groups_keys, groups_turns).reshape((TOKENS, GROUP_TOP))
    picks = picks_of(part_keys[2], TOKENS, GROUP_TOP * EXP_GROUP, TOP, 4096)
    gates = jnp.clip(jnp.exp(math.log(1.0) - 2.306499 * jax.random.uniform(part_keys[3], (TOKENS, TOP), jnp.float32) ** block_levels(part_keys[3], (TOKENS, TOP), ((0, 256),), -0.2, 0.2)), 0.099609375, 1.0).astype(jnp.bfloat16)
    w_gate = gaussian(splits[4], (N_GROUP, N_MEMBER, D, FF_DEV), D ** -0.5, 0.125, ((0, 16), (1, 16)))
    w_up = gaussian(splits[5], (N_GROUP, N_MEMBER, D, FF_DEV), D ** -0.5, 0.125, ((0, 16), (1, 16)))
    w_down = gaussian(splits[6], (N_GROUP, N_MEMBER, FF_DEV, D), FF ** -0.5, 0.21875, ((0, 16), (1, 16)))
    saved = gaussian(part_keys[7], (N_GROUP, N_MEMBER, SLOTS, D), 1.0, 6.0, ((0, 16), (1, 16)))
    return dict(out_grad=out_grad, groups=groups, picks=picks, gates=gates, w_gate=w_gate, w_up=w_up, w_down=w_down, saved=saved)


def expert_grad(inputs, grad_rows, w_gate, w_up, w_down):
    pre_gate = jnp.dot(inputs, w_gate, preferred_element_type=jnp.float32)
    pre_up = jnp.dot(inputs, w_up, preferred_element_type=jnp.float32)
    hidden_grad = lax.dot_general(grad_rows, w_down, (((1,), (1,)), ((), ())), preferred_element_type=jnp.float32)
    sigmoid_gate = jax.nn.sigmoid(pre_gate)
    gate_grad = (hidden_grad * pre_up * sigmoid_gate * (1.0 + pre_gate * (1.0 - sigmoid_gate))).astype(jnp.bfloat16)
    up_grad = (hidden_grad * pre_gate * sigmoid_gate).astype(jnp.bfloat16)
    input_part = lax.dot_general(gate_grad, w_gate, (((1,), (1,)), ((), ())), preferred_element_type=jnp.float32)
    input_part = input_part + lax.dot_general(up_grad, w_up, (((1,), (1,)), ((), ())), preferred_element_type=jnp.float32)
    return input_part.astype(jnp.bfloat16)

def reference(out_grad, groups, picks, gates, w_gate, w_up, w_down, saved):
    column = (picks // EXP_GROUP).astype(jnp.int32)
    expert_of = (jnp.take_along_axis(groups, column, axis=1) * EXP_GROUP + picks % EXP_GROUP).astype(jnp.int32)
    by_column = expert_of.reshape(N_GROUP, N_MEMBER, TOK_DEV, TOP).transpose(1, 0, 2, 3)
    by_column = by_column.reshape(N_MEMBER, N_GROUP * TOK_DEV, TOP)
    expert_ids = jnp.arange(EXPERTS, dtype=jnp.int32)
    hot = (by_column[:, :, :, None] == expert_ids).any(axis=2).astype(jnp.int32)
    before = jnp.cumsum(hot, axis=1) - hot
    rank_cols = jnp.take_along_axis(before, by_column, axis=2).astype(jnp.int32)
    ranking = rank_cols.reshape(N_MEMBER, N_GROUP, TOK_DEV, TOP).transpose(1, 0, 2, 3).reshape(TOKENS, TOP)
    member_col = jnp.arange(TOKENS, dtype=jnp.int32) // TOK_DEV % N_MEMBER
    retained = ranking < MEMBER_CAP
    slot = jnp.where(retained, member_col[:, None] * MEMBER_CAP + ranking, SLOTS).astype(jnp.int32)
    scaled = (gates.astype(jnp.float32)[:, :, None] * out_grad.astype(jnp.float32)[:, None, :]).astype(jnp.bfloat16)
    table = jnp.zeros((EXPERTS, SLOTS, D), jnp.bfloat16).at[expert_of, slot].set(scaled, mode='drop')
    gate_flat = w_gate.reshape(N_GROUP * N_MEMBER, D, FF_DEV)
    up_flat = w_up.reshape(N_GROUP * N_MEMBER, D, FF_DEV)
    down_flat = w_down.reshape(N_GROUP * N_MEMBER, FF_DEV, D)
    saved_flat = saved.reshape(N_GROUP * N_MEMBER, SLOTS, D)

    def one_half(device):
        expert = device // N_MEMBER * EXP_GROUP + device % N_MEMBER // 2
        return expert_grad(saved_flat[device], table[expert], gate_flat[device], up_flat[device], down_flat[device])
    parts = lax.map(one_half, jnp.arange(N_GROUP * N_MEMBER, dtype=jnp.int32))
    paired = parts.reshape(EXPERTS, 2, SLOTS, D)
    summed = paired[:, 0].astype(jnp.float32) + paired[:, 1].astype(jnp.float32)
    safe_slot = jnp.minimum(slot, SLOTS - 1).astype(jnp.int32)
    total = jnp.zeros((TOKENS, D), jnp.float32)
    for slot_col in range(3):
        group_sum = jnp.zeros((TOKENS, D), jnp.float32)
        for index_k in range(TOP):
            usable = (retained[:, index_k] & (column[:, index_k] == slot_col)).astype(jnp.float32)
            group_sum = group_sum + usable[:, None] * summed[expert_of[:, index_k], safe_slot[:, index_k]]
        rounded = lax.optimization_barrier(group_sum.astype(jnp.bfloat16))
        total = total + rounded.astype(jnp.float32)
    return total.astype(jnp.bfloat16)
```

```python
import jax
import jax.numpy as jnp
from jax import lax
from jax.experimental import pallas as pl
from jax.experimental.pallas import tpu as pltpu
from jax.sharding import PartitionSpec as P

LANES = 128
SUB = 8
WIDE = 16
F32 = jnp.float32
BF16 = jnp.bfloat16


def iota(shape, dim):
    return lax.broadcasted_iota(jnp.int32, shape, dim)


def dot(a, b, left=1, right=0):
    return lax.dot_general(
        a.astype(BF16), b.astype(BF16), (((left,), (right,)), ((), ())), preferred_element_type=F32
    )


def fold(rows):
    return rows.reshape(rows.shape[0], rows.shape[1] // LANES, LANES)


def unfold(rows):
    return rows.reshape(rows.shape[0], rows.shape[1] * LANES)


def pack_group(out_ref, main, ninth, extra):
    count, width = ninth.shape
    half = width // 2
    main = main.reshape(count, SUB, width)
    tiles = half // LANES
    for q in range(tiles):
        low = main[:, :, q * LANES : (q + 1) * LANES]
        high = main[:, :, half + q * LANES : half + (q + 1) * LANES]
        tile = jnp.concatenate([low, high], axis=1)
        out_ref[:, q * WIDE : (q + 1) * WIDE, :] = tile.astype(BF16)
    tail = out_ref.shape[1] - tiles * WIDE
    pad = tail - width // LANES - 1
    block = jnp.concatenate(
        [fold(ninth), extra.reshape(count, 1, LANES), jnp.zeros((count, pad, LANES), F32)], axis=1
    )
    out_ref[:, tiles * WIDE :, :] = block.astype(BF16)


def unpack_group(in_ref, width):
    count = in_ref.shape[0]
    tiles = width // 2 // LANES
    low, high = [], []
    for q in range(tiles):
        tile = in_ref[:, q * WIDE : (q + 1) * WIDE, :].astype(F32)
        low.append(tile[:, :SUB, :].reshape(count * SUB, LANES).astype(BF16))
        high.append(tile[:, SUB:, :].reshape(count * SUB, LANES).astype(BF16))
    main = jnp.concatenate(low + high, axis=1)
    block = in_ref[:, tiles * WIDE :, :].astype(F32)
    ninth = unfold(block[:, : width // LANES, :])
    extra = block[:, width // LANES, :]
    return main, ninth.astype(BF16), extra


def pack_member(out_ref, main, last):
    count = out_ref.shape[0]
    width = main.shape[1]
    tiles = width // LANES
    main = main.astype(BF16).reshape(count, WIDE, width)
    for q in range(tiles):
        out_ref[:, q * WIDE : (q + 1) * WIDE, :] = main[:, :, q * LANES : (q + 1) * LANES]
    room = (out_ref.shape[1] - tiles * WIDE) // 2
    pad = jnp.zeros((count, room - tiles, LANES), F32)
    last = fold(last)
    block = jnp.concatenate([last[:count], pad, last[count:], pad], axis=1)
    out_ref[:, tiles * WIDE :, :] = block.astype(BF16)


def unpack_member(in_ref, width):
    count = in_ref.shape[0]
    tiles = width // LANES
    main = [in_ref[:, q * WIDE : (q + 1) * WIDE, :].reshape(count * WIDE, LANES) for q in range(tiles)]
    main = jnp.concatenate(main, axis=1)
    room = (in_ref.shape[1] - tiles * WIDE) // 2
    block = in_ref[:, tiles * WIDE :, :].astype(F32)
    last = [unfold(block[:, s * room : s * room + tiles, :]) for s in range(2)]
    return main, jnp.concatenate(last, axis=0).astype(BF16)


def columns(rows):
    count = rows.shape[1]
    eye = (iota((count, count), 0) == iota((count, count), 1)).astype(F32)
    return dot(eye, rows.astype(F32), 1, 1)


def place(groups, tok_count, group_count):
    hit = groups[:, 0:1] == iota((tok_count, group_count), 1)
    for k in range(1, 3):
        hit = hit | (groups[:, k : k + 1] == iota((tok_count, group_count), 1))
    hit = hit.astype(F32)
    earlier = (iota((tok_count, tok_count), 1) < iota((tok_count, tok_count), 0)).astype(F32)
    position = jnp.where(hit > 0, dot(earlier, hit), 99.0)
    rows = group_count * SUB
    spread = (iota((rows, group_count), 0) >> 3 == iota((rows, group_count), 1)).astype(F32)
    at = dot(spread, position, 1, 1)
    main = (at == (iota((rows, tok_count), 0) & 7).astype(F32)).astype(F32)
    eye = (iota((group_count, group_count), 0) == iota((group_count, group_count), 1)).astype(F32)
    ninth = (dot(eye, position, 1, 1) == float(SUB)).astype(F32)
    return main, ninth, spread


def send_kernel(grad_ref, groups_ref, picks_ref, gates_ref, out_ref, *, group_count):
    tok_count = grad_ref.shape[0]
    groups = columns(groups_ref[...]).astype(jnp.int32)
    picks = columns(picks_ref[...]).astype(jnp.int32)
    gates = columns(gates_ref[...])
    main, ninth, spread = place(groups, tok_count, group_count)
    table = jnp.zeros((tok_count, LANES), F32)
    for k in range(picks.shape[1]):
        pick = picks[:, k : k + 1]
        column = pick >> 3
        group = jnp.where(
            column == 0, groups[:, 0:1], jnp.where(column == 1, groups[:, 1:2], groups[:, 2:3])
        )
        expert = group * SUB + (pick & 7)
        table = table + jnp.where(expert == iota((tok_count, LANES), 1), gates[:, k : k + 1], 0.0)
    rows = group_count * SUB
    lane_of = iota((rows, LANES), 1)
    row_of = iota((rows, LANES), 0)
    same_within = ((iota((LANES, LANES), 0) & 7) == (iota((LANES, LANES), 1) & 7)).astype(F32)
    of_row = jnp.where(row_of >> 3 == lane_of >> 3, dot(main, table), 0.0)
    of_row = jnp.where((row_of & 7) == lane_of >> 3, dot(of_row, same_within), 0.0)
    extra = dot(spread, of_row, 0, 0)
    lane_of = iota((group_count, LANES), 1)
    of_row = jnp.where(iota((group_count, LANES), 0) == lane_of >> 3, dot(ninth, table), 0.0)
    extra = extra + jnp.where(lane_of >> 3 == SUB, dot(of_row, same_within), 0.0)
    grad = grad_ref[...]
    pack_group(out_ref, dot(main, grad), dot(ninth, grad), extra)


def route_kernel(in_ref, out_ref, main_ref, ninth_ref, *, width, cap):
    count, experts = in_ref.shape[0], SUB
    rows = count * SUB
    main, ninth, extra = unpack_group(in_ref, width)
    spread = (iota((count, rows), 1) >> 3 == iota((count, rows), 0)).astype(F32)
    wide = dot(extra, spread, 0, 0)
    wide = jnp.where(iota((LANES, rows), 0) >> 3 == (iota((LANES, rows), 1) & 7), wide, 0.0)
    pick = ((iota((experts, LANES), 1) & 7) == iota((experts, LANES), 0)).astype(F32)
    gate = dot(pick, wide)
    pick = (iota((experts, LANES), 1) == iota((experts, LANES), 0) + SUB * SUB).astype(F32)
    gate9 = dot(pick, extra, 1, 1)
    on, on9 = (gate > 0).astype(F32), (gate9 > 0).astype(F32)
    mm = (iota((rows, rows), 0) < iota((rows, rows), 1)).astype(F32)
    nm = (iota((count, rows), 0) < iota((count, rows), 1) >> 3).astype(F32)
    mn = (iota((rows, count), 0) >> 3 <= iota((rows, count), 1)).astype(F32)
    nn = (iota((count, count), 0) < iota((count, count), 1)).astype(F32)
    rank = dot(on, mm) + dot(on9, nm)
    rank9 = dot(on, mn) + dot(on9, nn)

    def weights(expert_of, slot_of):
        slots = expert_of.shape[0]
        expand = (expert_of[:, :experts] == iota((slots, experts), 1)).astype(F32)

        def one(rank, gate):
            slot = slot_of[:, : rank.shape[1]].astype(F32)
            value = dot(expand, gate)
            return jnp.where((dot(expand, rank) == slot) & (value > 0), value, 0.0)

        return one(rank, gate), one(rank9, gate9)

    big = iota((experts * WIDE, LANES), 0)
    small = iota((2 * experts, LANES), 0)
    weigh, weigh9 = weights(big >> 4, big & 15)
    last, last9 = weights(small & 7, WIDE + (small >> 3))
    first = dot(weigh, main) + dot(weigh9, ninth)
    second = dot(last, main) + dot(last9, ninth)
    pack_member(out_ref, first, second)
    main_ref[: experts * WIDE, :] = (weigh > 0).astype(F32).astype(BF16)
    main_ref[experts * WIDE :, :] = (last > 0).astype(F32).astype(BF16)
    ninth_ref[: experts * WIDE, :] = (weigh9 > 0).astype(F32).astype(BF16)
    ninth_ref[experts * WIDE :, :] = (last9 > 0).astype(F32).astype(BF16)


def expert_kernel(
    in_ref, factor_ref, factor2_ref, down_hbm, down2_hbm, gate_hbm, up_hbm, gate2_hbm, up2_hbm, out_ref,
    down_ref, down2_ref, gate_ref, up_ref, gate2_ref, up2_ref, sems,
):
    hidden, width = down_ref.shape
    sources = (down_hbm, down2_hbm, gate_hbm, up_hbm, gate2_hbm, up2_hbm)
    weights = (down_ref, down2_ref, gate_ref, up_ref, gate2_ref, up2_ref)
    copies = [
        pltpu.make_async_copy(source, weight, sems.at[i])
        for i, (source, weight) in enumerate(zip(sources, weights))
    ]
    for copy in copies:
        copy.start()
    main, last = unpack_member(in_ref, width)
    split = main.shape[0]
    rows = jnp.concatenate([main, last], axis=0)
    sides = []
    for i, factor in enumerate((factor_ref, factor2_ref)):
        copies[i].wait()
        grad = dot(rows, weights[i][...], 1, 1)
        sides.append((grad * factor[:, :hidden]).astype(BF16))
        sides.append((grad * factor[:, hidden:]).astype(BF16))
    for copy in copies[2:]:
        copy.wait()
    blocks = []
    step = width // 5
    for block in range(5):
        at = slice(block * step, (block + 1) * step)
        total = dot(sides[0], gate_ref[at, :], 1, 1)
        for side, weight in zip(sides[1:], (up_ref, gate2_ref, up2_ref)):
            total = total + dot(side, weight[at, :], 1, 1)
        blocks.append(total)
    parts = jnp.concatenate(blocks, axis=1)
    pack_member(out_ref, parts[:split], parts[split:])


def gather_kernel(in_ref, main_ref, ninth_ref, out_ref, *, width):
    main, last = unpack_member(in_ref, width)
    split = main.shape[0]
    total = dot(main_ref[:split, :], main, 0, 0) + dot(main_ref[split:, :], last, 0, 0)
    total9 = dot(ninth_ref[:split, :], main, 0, 0) + dot(ninth_ref[split:, :], last, 0, 0)
    pack_group(out_ref, total, total9, jnp.zeros((out_ref.shape[0], LANES), F32))


def final_kernel(in_ref, groups_ref, out_ref):
    tok_count, width = out_ref.shape
    groups = columns(groups_ref[...]).astype(jnp.int32)
    main, ninth, _ = place(groups, tok_count, in_ref.shape[0])
    rows, rows9, _ = unpack_group(in_ref, width)
    out_ref[...] = (dot(main, rows, 0, 0) + dot(ninth, rows9, 0, 0)).astype(BF16)


def call(kernel, outs, *args):
    shapes = [jax.ShapeDtypeStruct(shape, BF16) for shape in outs]
    return pl.pallas_call(
        kernel,
        out_shape=shapes if len(shapes) > 1 else shapes[0],
        compiler_params=pltpu.CompilerParams(vmem_limit_bytes=32 * 1024 * 1024),
    )(*args)


def expert_parts(rows, *weights):
    vmem, anywhere = pl.BlockSpec(memory_space=pltpu.VMEM), pl.BlockSpec(memory_space=pl.ANY)
    matrices = weights[2:]
    return pl.pallas_call(
        expert_kernel,
        out_shape=jax.ShapeDtypeStruct(rows.shape, BF16),
        in_specs=[vmem] * 3 + [anywhere] * 6,
        out_specs=vmem,
        scratch_shapes=[pltpu.VMEM(weight.shape, BF16) for weight in matrices]
        + [pltpu.SemaphoreType.DMA((len(matrices),))],
        compiler_params=pltpu.CompilerParams(vmem_limit_bytes=40 * 1024 * 1024),
    )(rows, *weights)


def body(out_grad, groups, picks, gates, w_gate, w_up, w_down, saved):
    group_count = lax.axis_size("group")
    member_count = lax.axis_size("member")
    experts = member_count // 2
    tok_count, width = out_grad.shape
    cap = 12 * tok_count // member_count
    slots = experts * cap
    hidden = w_gate.shape[-1]
    same_core = [list(range(c, member_count, 2)) for c in range(2)]
    swap = [(i, i ^ 1) for i in range(member_count)]
    core = lax.axis_index("member") % 2
    group_shape = (group_count, width * SUB // LANES + 24, LANES)
    member_shape = (experts, width * WIDE // LANES + 48, LANES)

    def over_group(rows):
        return lax.all_to_all(rows, "group", split_axis=0, concat_axis=0, tiled=True)

    def over_member(rows):
        return lax.all_to_all(
            rows, "member", split_axis=0, concat_axis=0, axis_index_groups=same_core, tiled=True
        )

    def across(rows):
        return lax.ppermute(rows, "member", swap)

    def send(*args):
        return call(lambda *refs: send_kernel(*refs, group_count=group_count), [group_shape], *args)

    payload = send(out_grad, groups.T, picks.T, gates.T)
    arrived = over_group(payload)

    w_gate, w_up, w_down, inputs = w_gate[0, 0], w_up[0, 0], w_down[0, 0], saved[0, 0]
    _, inputs = lax.optimization_barrier((payload, inputs))
    pre_gate = jnp.dot(inputs, w_gate, preferred_element_type=F32)
    pre_up = jnp.dot(inputs, w_up, preferred_element_type=F32)
    pre_gate, pre_up, *sent = lax.optimization_barrier((pre_gate, pre_up, w_down, w_gate, w_up))
    w_down2, w_gate2, w_up2 = [across(weight) for weight in sent]
    gate = jax.nn.sigmoid(pre_gate)
    factors = jnp.concatenate(
        [pre_up * gate * (1.0 + pre_gate * (1.0 - gate)), pre_gate * gate], axis=1
    )
    factors = factors.reshape(experts, 2, cap, 2 * hidden)
    mine = jnp.where(core == 0, factors[:, 0], factors[:, 1])
    yours = jnp.where(core == 0, factors[:, 1], factors[:, 0])

    def slot_order(values):
        first = values[:, :WIDE].reshape(experts * WIDE, 2 * hidden)
        second = values[:, WIDE:].transpose(1, 0, 2).reshape(experts * 2, 2 * hidden)
        return jnp.concatenate([first, second], axis=0)

    mine, yours = slot_order(mine), across(slot_order(yours))

    def route(rows):
        kernel = lambda *refs: route_kernel(*refs, width=width, cap=cap)
        return call(
            kernel, [member_shape, (slots, group_count * SUB), (slots, group_count)], rows
        )

    scaled, routing, routing9 = route(arrived)
    weights = (mine, yours, w_down, w_down2, w_gate, w_up, w_gate2, w_up2)
    scaled, *weights = lax.optimization_barrier((scaled,) + weights)
    returned = over_member(expert_parts(over_member(scaled), *weights))
    sums = call(
        lambda *refs: gather_kernel(*refs, width=width),
        [group_shape],
        returned,
        routing,
        routing9,
    )
    return call(final_kernel, [(tok_count, width)], over_group(sums), groups.T)


def solution(mesh):
    token = P(("dp", "group", "member"), None)
    weight = P("group", "member", None, None)
    return jax.shard_map(
        body,
        mesh=mesh,
        in_specs=(token,) * 4 + (weight,) * 3 + (P("group", "member", "dp", None),),
        out_specs=token,
        check_vma=False,
    )
```

```python
import jax
import jax.numpy as jnp
from jax import lax
from jax.experimental import pallas as pl
from jax.experimental.pallas import tpu as pltpu
from jax.sharding import PartitionSpec as P

LANES = 128
SUB = 8
WIDE = 16
F32 = jnp.float32
BF16 = jnp.bfloat16


def iota(shape, dim):
    return lax.broadcasted_iota(jnp.int32, shape, dim)


def dot(a, b, left=1, right=0):
    return lax.dot_general(
        a.astype(BF16), b.astype(BF16), (((left,), (right,)), ((), ())), preferred_element_type=F32
    )


def fold(rows):
    return rows.reshape(rows.shape[0], rows.shape[1] // LANES, LANES)


def unfold(rows):
    return rows.reshape(rows.shape[0], rows.shape[1] * LANES)


def pack_group(out_ref, main, ninth, extra):
    count, width = ninth.shape
    half = width // 2
    main = main.reshape(count, SUB, width)
    tiles = half // LANES
    for q in range(tiles):
        low = main[:, :, q * LANES : (q + 1) * LANES]
        high = main[:, :, half + q * LANES : half + (q + 1) * LANES]
        tile = jnp.concatenate([low, high], axis=1)
        out_ref[:, q * WIDE : (q + 1) * WIDE, :] = tile.astype(BF16)
    tail = out_ref.shape[1] - tiles * WIDE
    pad = tail - width // LANES - 1
    block = jnp.concatenate(
        [fold(ninth), extra.reshape(count, 1, LANES), jnp.zeros((count, pad, LANES), F32)], axis=1
    )
    out_ref[:, tiles * WIDE :, :] = block.astype(BF16)


def unpack_group(in_ref, width):
    count = in_ref.shape[0]
    tiles = width // 2 // LANES
    low, high = [], []
    for q in range(tiles):
        tile = in_ref[:, q * WIDE : (q + 1) * WIDE, :].astype(F32)
        low.append(tile[:, :SUB, :].reshape(count * SUB, LANES).astype(BF16))
        high.append(tile[:, SUB:, :].reshape(count * SUB, LANES).astype(BF16))
    main = jnp.concatenate(low + high, axis=1)
    block = in_ref[:, tiles * WIDE :, :].astype(F32)
    ninth = unfold(block[:, : width // LANES, :])
    extra = block[:, width // LANES, :]
    return main, ninth.astype(BF16), extra


def pack_member(out_ref, main, last):
    count = out_ref.shape[0]
    width = main.shape[1]
    tiles = width // LANES
    main = main.astype(BF16).reshape(count, WIDE, width)
    for q in range(tiles):
        out_ref[:, q * WIDE : (q + 1) * WIDE, :] = main[:, :, q * LANES : (q + 1) * LANES]
    room = (out_ref.shape[1] - tiles * WIDE) // 2
    pad = jnp.zeros((count, room - tiles, LANES), F32)
    last = fold(last)
    block = jnp.concatenate([last[:count], pad, last[count:], pad], axis=1)
    out_ref[:, tiles * WIDE :, :] = block.astype(BF16)


def unpack_member(in_ref, width):
    count = in_ref.shape[0]
    tiles = width // LANES
    main = [in_ref[:, q * WIDE : (q + 1) * WIDE, :].reshape(count * WIDE, LANES) for q in range(tiles)]
    main = jnp.concatenate(main, axis=1)
    room = (in_ref.shape[1] - tiles * WIDE) // 2
    block = in_ref[:, tiles * WIDE :, :].astype(F32)
    last = [unfold(block[:, s * room : s * room + tiles, :]) for s in range(2)]
    return main, jnp.concatenate(last, axis=0).astype(BF16)


def columns(rows):
    count = rows.shape[1]
    eye = (iota((count, count), 0) == iota((count, count), 1)).astype(F32)
    return dot(eye, rows.astype(F32), 1, 1)


def place(groups, tok_count, group_count):
    hit = groups[:, 0:1] == iota((tok_count, group_count), 1)
    for k in range(1, 3):
        hit = hit | (groups[:, k : k + 1] == iota((tok_count, group_count), 1))
    hit = hit.astype(F32)
    earlier = (iota((tok_count, tok_count), 1) < iota((tok_count, tok_count), 0)).astype(F32)
    position = jnp.where(hit > 0, dot(earlier, hit), 99.0)
    rows = group_count * SUB
    spread = (iota((rows, group_count), 0) >> 3 == iota((rows, group_count), 1)).astype(F32)
    at = dot(spread, position, 1, 1)
    main = (at == (iota((rows, tok_count), 0) & 7).astype(F32)).astype(F32)
    eye = (iota((group_count, group_count), 0) == iota((group_count, group_count), 1)).astype(F32)
    ninth = (dot(eye, position, 1, 1) == float(SUB)).astype(F32)
    return main, ninth, spread


def send_kernel(
    grad_hbm, groups_hbm, picks_hbm, gates_hbm, out_ref, grad_ref, groups_ref, picks_ref, gates_ref, sems,
    *, group_count,
):
    pairs = (
        (groups_hbm, groups_ref), (picks_hbm, picks_ref), (gates_hbm, gates_ref), (grad_hbm, grad_ref)
    )
    copies = [pltpu.make_async_copy(a, b, sems.at[i]) for i, (a, b) in enumerate(pairs)]
    for copy in copies:
        copy.start()
    for copy in copies[:3]:
        copy.wait()
    tok_count = grad_ref.shape[0]
    groups = columns(groups_ref[...]).astype(jnp.int32)
    picks = columns(picks_ref[...]).astype(jnp.int32)
    gates = columns(gates_ref[...])
    main, ninth, spread = place(groups, tok_count, group_count)
    table = jnp.zeros((tok_count, LANES), F32)
    for k in range(picks.shape[1]):
        pick = picks[:, k : k + 1]
        column = pick >> 3
        group = jnp.where(
            column == 0, groups[:, 0:1], jnp.where(column == 1, groups[:, 1:2], groups[:, 2:3])
        )
        expert = group * SUB + (pick & 7)
        table = table + jnp.where(expert == iota((tok_count, LANES), 1), gates[:, k : k + 1], 0.0)
    rows = group_count * SUB
    lane_of = iota((rows, LANES), 1)
    row_of = iota((rows, LANES), 0)
    same_within = ((iota((LANES, LANES), 0) & 7) == (iota((LANES, LANES), 1) & 7)).astype(F32)
    of_row = jnp.where(row_of >> 3 == lane_of >> 3, dot(main, table), 0.0)
    of_row = jnp.where((row_of & 7) == lane_of >> 3, dot(of_row, same_within), 0.0)
    extra = dot(spread, of_row, 0, 0)
    lane_of = iota((group_count, LANES), 1)
    of_row = jnp.where(iota((group_count, LANES), 0) == lane_of >> 3, dot(ninth, table), 0.0)
    extra = extra + jnp.where(lane_of >> 3 == SUB, dot(of_row, same_within), 0.0)
    copies[3].wait()
    grad = grad_ref[...]
    pack_group(out_ref, dot(main, grad), dot(ninth, grad), extra)


def route_kernel(in_ref, out_ref, main_ref, ninth_ref, *, width, cap):
    count, experts = in_ref.shape[0], SUB
    rows = count * SUB
    main, ninth, extra = unpack_group(in_ref, width)
    spread = (iota((count, rows), 1) >> 3 == iota((count, rows), 0)).astype(F32)
    wide = dot(extra, spread, 0, 0)
    wide = jnp.where(iota((LANES, rows), 0) >> 3 == (iota((LANES, rows), 1) & 7), wide, 0.0)
    pick = ((iota((experts, LANES), 1) & 7) == iota((experts, LANES), 0)).astype(F32)
    gate = dot(pick, wide)
    pick = (iota((experts, LANES), 1) == iota((experts, LANES), 0) + SUB * SUB).astype(F32)
    gate9 = dot(pick, extra, 1, 1)
    on, on9 = (gate > 0).astype(F32), (gate9 > 0).astype(F32)
    mm = (iota((rows, rows), 0) < iota((rows, rows), 1)).astype(F32)
    nm = (iota((count, rows), 0) < iota((count, rows), 1) >> 3).astype(F32)
    mn = (iota((rows, count), 0) >> 3 <= iota((rows, count), 1)).astype(F32)
    nn = (iota((count, count), 0) < iota((count, count), 1)).astype(F32)
    rank = dot(on, mm) + dot(on9, nm)
    rank9 = dot(on, mn) + dot(on9, nn)

    def weights(expert_of, slot_of):
        slots = expert_of.shape[0]
        expand = (expert_of[:, :experts] == iota((slots, experts), 1)).astype(F32)

        def one(rank, gate):
            slot = slot_of[:, : rank.shape[1]].astype(F32)
            value = dot(expand, gate)
            return jnp.where((dot(expand, rank) == slot) & (value > 0), value, 0.0)

        return one(rank, gate), one(rank9, gate9)

    big = iota((experts * WIDE, LANES), 0)
    small = iota((2 * experts, LANES), 0)
    weigh, weigh9 = weights(big >> 4, big & 15)
    last, last9 = weights(small & 7, WIDE + (small >> 3))
    first = dot(weigh, main) + dot(weigh9, ninth)
    second = dot(last, main) + dot(last9, ninth)
    pack_member(out_ref, first, second)
    main_ref[: experts * WIDE, :] = (weigh > 0).astype(F32).astype(BF16)
    main_ref[experts * WIDE :, :] = (last > 0).astype(F32).astype(BF16)
    ninth_ref[: experts * WIDE, :] = (weigh9 > 0).astype(F32).astype(BF16)
    ninth_ref[experts * WIDE :, :] = (last9 > 0).astype(F32).astype(BF16)


def prepare_kernel(flags_ref, *refs, cap):
    saved_hbm, gate_hbm, up_hbm, down_hbm = refs[:4]
    outs, scratch, sems = refs[-16:-11], refs[-11:-1], refs[-1]
    saved_ref, gate_ref, up_ref, down_ref, mine_ref, yours_ref, gate_t, up_t, down_t, _ = scratch

    @pl.when(flags_ref[0] == 1)
    def _():
        pairs = zip((saved_hbm, gate_hbm, up_hbm, down_hbm), (saved_ref, gate_ref, up_ref, down_ref))
        loads = [pltpu.make_async_copy(a, b, sems.at[i]) for i, (a, b) in enumerate(pairs)]
        results = (mine_ref, yours_ref, gate_t, up_t, down_t)
        stores = [
            pltpu.make_async_copy(a, b, sems.at[4 + i]) for i, (a, b) in enumerate(zip(results, outs))
        ]
        for load in loads:
            load.start()
        slots = saved_ref.shape[0]
        half = slots // 2
        experts = half // cap
        core = flags_ref[1]
        row = iota((slots, slots), 0)
        column = jnp.where(row < half, core, 1 - core)
        row = jnp.where(row < half, row, row - half)
        late = row - experts * WIDE
        member = jnp.where(late < 0, row >> 4, late & 7)
        place_in = jnp.where(late < 0, row & 15, WIDE + (late >> 3))
        order = iota((slots, slots), 1) == (2 * member + column) * cap + place_in
        loads[0].wait()
        rows = dot(order.astype(F32), saved_ref[...]).astype(BF16)
        loads[1].wait()
        pre_gate = dot(rows, gate_ref[...])
        loads[2].wait()
        pre_up = dot(rows, up_ref[...])
        gate = 1.0 / (1.0 + jnp.exp(-pre_gate))
        first = pre_up * gate * (1.0 + pre_gate * (1.0 - gate))
        factors = jnp.concatenate([first, pre_gate * gate], axis=1)
        mine_ref[...] = factors[:half]
        yours_ref[...] = factors[half:]
        stores[0].start()
        stores[1].start()
        gate_t[...] = gate_ref[...].T
        stores[2].start()
        up_t[...] = up_ref[...].T
        stores[3].start()
        loads[3].wait()
        down_t[...] = down_ref[...].T
        stores[4].start()
        for store in stores:
            store.wait()


def prepare(flags, inputs, earlier, cap):
    saved, gate, up, down = inputs
    slots, hidden = saved.shape[0], gate.shape[1]
    factor = jax.ShapeDtypeStruct((slots // 2, 2 * hidden), F32)
    outs = [factor, factor] + [
        jax.ShapeDtypeStruct(weight.shape[::-1], BF16) for weight in (gate, up, down)
    ]
    return pl.pallas_call(
        lambda *refs: prepare_kernel(*refs, cap=cap),
        out_shape=[pltpu.HBM(x.shape, x.dtype) for x in outs],
        in_specs=[pl.BlockSpec(memory_space=pltpu.SMEM)] + [HBM] * (4 + len(earlier)),
        out_specs=[HBM] * len(outs),
        scratch_shapes=[pltpu.VMEM(x.shape, x.dtype) for x in (*inputs, *outs)]
        + [pltpu.VMEM((SUB, LANES), F32), pltpu.SemaphoreType.DMA((9,))],
        input_output_aliases={5 + i: i for i in range(len(earlier))},
        cost_estimate=pl.CostEstimate(flops=6 * 10**9, bytes_accessed=20 * 10**6, transcendentals=0),
        compiler_params=pltpu.CompilerParams(vmem_limit_bytes=40 * 1024 * 1024),
    )(flags, *in_hbm(inputs), *in_hbm(earlier))


def expert_kernel(
    in_ref, factor_ref, factor2_ref, down_hbm, down2_hbm, gate_hbm, up_hbm, gate2_hbm, up2_hbm, out_ref,
    down_ref, down2_ref, gate_ref, up_ref, gate2_ref, up2_ref, sems,
):
    width, hidden = down_ref.shape
    sources = (down_hbm, down2_hbm, gate_hbm, up_hbm, gate2_hbm, up2_hbm)
    weights = (down_ref, down2_ref, gate_ref, up_ref, gate2_ref, up2_ref)
    copies = [
        pltpu.make_async_copy(source, weight, sems.at[i])
        for i, (source, weight) in enumerate(zip(sources, weights))
    ]
    for copy in copies:
        copy.start()
    main, last = unpack_member(in_ref, width)
    split = main.shape[0]
    rows = jnp.concatenate([main, last], axis=0)
    sides = []
    for i, factor in enumerate((factor_ref, factor2_ref)):
        copies[i].wait()
        grad = dot(rows, weights[i][...])
        sides.append((grad * factor[:, :hidden]).astype(BF16))
        sides.append((grad * factor[:, hidden:]).astype(BF16))
    for copy in copies[2:]:
        copy.wait()
    parts = dot(sides[0], gate_ref[...])
    for side, weight in zip(sides[1:], (up_ref, gate2_ref, up2_ref)):
        parts = parts + dot(side, weight[...])
    pack_member(out_ref, parts[:split], parts[split:])


def gather_kernel(in_ref, main_ref, ninth_ref, out_ref, *, width):
    main, last = unpack_member(in_ref, width)
    split = main.shape[0]
    total = dot(main_ref[:split, :], main, 0, 0) + dot(main_ref[split:, :], last, 0, 0)
    total9 = dot(ninth_ref[:split, :], main, 0, 0) + dot(ninth_ref[split:, :], last, 0, 0)
    pack_group(out_ref, total, total9, jnp.zeros((out_ref.shape[0], LANES), F32))


def final_kernel(in_ref, groups_ref, out_ref):
    tok_count, width = out_ref.shape
    groups = columns(groups_ref[...]).astype(jnp.int32)
    main, ninth, _ = place(groups, tok_count, in_ref.shape[0])
    rows, rows9, _ = unpack_group(in_ref, width)
    out_ref[...] = (dot(main, rows, 0, 0) + dot(ninth, rows9, 0, 0)).astype(BF16)


HBM = pl.BlockSpec(memory_space=pltpu.HBM)
VMEM = pl.BlockSpec(memory_space=pltpu.VMEM)


def in_hbm(arrays):
    return [pltpu.with_memory_space_constraint(x, pltpu.HBM) for x in arrays]


def call(kernel, outs, *args):
    shapes = [jax.ShapeDtypeStruct(shape, BF16) for shape in outs]
    return pl.pallas_call(
        kernel,
        out_shape=shapes if len(shapes) > 1 else shapes[0],
        compiler_params=pltpu.CompilerParams(vmem_limit_bytes=32 * 1024 * 1024),
    )(*args)


def expert_parts(rows, *weights):
    factors, matrices = weights[:2], in_hbm(weights[2:])
    return pl.pallas_call(
        expert_kernel,
        out_shape=jax.ShapeDtypeStruct(rows.shape, BF16),
        in_specs=[VMEM] * 3 + [HBM] * 6,
        out_specs=VMEM,
        scratch_shapes=[pltpu.VMEM(weight.shape, BF16) for weight in matrices]
        + [pltpu.SemaphoreType.DMA((len(matrices),))],
        compiler_params=pltpu.CompilerParams(vmem_limit_bytes=40 * 1024 * 1024),
    )(rows, *factors, *matrices)


def body(out_grad, groups, picks, gates, w_gate, w_up, w_down, saved):
    group_count = lax.axis_size("group")
    member_count = lax.axis_size("member")
    experts = member_count // 2
    tok_count, width = out_grad.shape
    cap = 12 * tok_count // member_count
    slots = experts * cap
    same_core = [list(range(c, member_count, 2)) for c in range(2)]
    swap = [(i, i ^ 1) for i in range(member_count)]
    core = lax.axis_index("member") % 2
    group_shape = (group_count, width * SUB // LANES + 24, LANES)
    member_shape = (experts, width * WIDE // LANES + 48, LANES)

    def over_group(rows):
        return lax.all_to_all(rows, "group", split_axis=0, concat_axis=0, tiled=True)

    def over_member(rows):
        return lax.all_to_all(
            rows, "member", split_axis=0, concat_axis=0, axis_index_groups=same_core, tiled=True
        )

    def across(rows):
        return lax.ppermute(rows, "member", swap)

    def send(*args):
        return pl.pallas_call(
            lambda *refs: send_kernel(*refs, group_count=group_count),
            out_shape=jax.ShapeDtypeStruct(group_shape, BF16),
            in_specs=[HBM] * len(args),
            out_specs=VMEM,
            scratch_shapes=[pltpu.VMEM(arg.shape, arg.dtype) for arg in args]
            + [pltpu.SemaphoreType.DMA((len(args),))],
            compiler_params=pltpu.CompilerParams(vmem_limit_bytes=32 * 1024 * 1024),
        )(*in_hbm(args))

    w_gate, w_up, w_down, inputs = w_gate[0, 0], w_up[0, 0], w_down[0, 0], saved[0, 0]
    inputs = (inputs, w_gate, w_up, w_down)
    payload = send(out_grad, groups.T, picks.T, gates.T)
    payload, *inputs = lax.optimization_barrier((payload, *inputs))
    earlier = prepare(jnp.stack([core, core]).astype(jnp.int32), inputs, (), cap)
    payload, *earlier = lax.optimization_barrier((payload, *earlier))
    arrived = over_group(payload)
    prepared = prepare(jnp.stack([1 - core, core]).astype(jnp.int32), inputs, tuple(earlier), cap)
    mine, yours, w_gate, w_up, w_down = prepared
    yours, w_down2, w_gate2, w_up2 = [across(x) for x in (yours, w_down, w_gate, w_up)]

    def route(rows):
        kernel = lambda *refs: route_kernel(*refs, width=width, cap=cap)
        return call(
            kernel, [member_shape, (slots, group_count * SUB), (slots, group_count)], rows
        )

    scaled, routing, routing9 = route(arrived)
    weights = (mine, yours, w_down, w_down2, w_gate, w_up, w_gate2, w_up2)
    scaled, *weights = lax.optimization_barrier((scaled,) + weights)
    returned = over_member(expert_parts(over_member(scaled), *weights))
    sums = call(
        lambda *refs: gather_kernel(*refs, width=width),
        [group_shape],
        returned,
        routing,
        routing9,
    )
    return call(final_kernel, [(tok_count, width)], over_group(sums), groups.T)


def solution(mesh):
    token = P(("dp", "group", "member"), None)
    weight = P("group", "member", None, None)
    return jax.shard_map(
        body,
        mesh=mesh,
        in_specs=(token,) * 4 + (weight,) * 3 + (P("group", "member", "dp", None),),
        out_specs=token,
        check_vma=False,
    )
```

```python
import jax
import jax.numpy as jnp
from jax import lax
from jax.experimental import pallas as pl
from jax.experimental.pallas import tpu as pltpu
from jax.sharding import PartitionSpec as P

LANES = 128
SUB = 8
WIDE = 16
F32 = jnp.float32
BF16 = jnp.bfloat16


def iota(shape, dim):
    return lax.broadcasted_iota(jnp.int32, shape, dim)


def dot(a, b, left=1, right=0):
    return lax.dot_general(
        a.astype(BF16), b.astype(BF16), (((left,), (right,)), ((), ())), preferred_element_type=F32
    )


def fold(rows):
    return rows.reshape(rows.shape[0], rows.shape[1] // LANES, LANES)


def unfold(rows):
    return rows.reshape(rows.shape[0], rows.shape[1] * LANES)


def pack_group(out_ref, main, ninth, extra):
    count, width = ninth.shape
    half = width // 2
    main = main.reshape(count, SUB, width)
    tiles = half // LANES
    for q in range(tiles):
        low = main[:, :, q * LANES : (q + 1) * LANES]
        high = main[:, :, half + q * LANES : half + (q + 1) * LANES]
        tile = jnp.concatenate([low, high], axis=1)
        out_ref[:, q * WIDE : (q + 1) * WIDE, :] = tile.astype(BF16)
    tail = out_ref.shape[1] - tiles * WIDE
    pad = tail - width // LANES - 1
    block = jnp.concatenate(
        [fold(ninth), extra.reshape(count, 1, LANES), jnp.zeros((count, pad, LANES), F32)], axis=1
    )
    out_ref[:, tiles * WIDE :, :] = block.astype(BF16)


def unpack_group(in_ref, width):
    count = in_ref.shape[0]
    tiles = width // 2 // LANES
    low, high = [], []
    for q in range(tiles):
        tile = in_ref[:, q * WIDE : (q + 1) * WIDE, :].astype(F32)
        low.append(tile[:, :SUB, :].reshape(count * SUB, LANES).astype(BF16))
        high.append(tile[:, SUB:, :].reshape(count * SUB, LANES).astype(BF16))
    main = jnp.concatenate(low + high, axis=1)
    block = in_ref[:, tiles * WIDE :, :].astype(F32)
    ninth = unfold(block[:, : width // LANES, :])
    extra = block[:, width // LANES, :]
    return main, ninth.astype(BF16), extra


def pack_member(out_ref, main, last):
    count = out_ref.shape[0]
    width = main.shape[1]
    tiles = width // LANES
    main = main.astype(BF16).reshape(count, WIDE, width)
    for q in range(tiles):
        out_ref[:, q * WIDE : (q + 1) * WIDE, :] = main[:, :, q * LANES : (q + 1) * LANES]
    room = (out_ref.shape[1] - tiles * WIDE) // 2
    pad = jnp.zeros((count, room - tiles, LANES), F32)
    last = fold(last)
    block = jnp.concatenate([last[:count], pad, last[count:], pad], axis=1)
    out_ref[:, tiles * WIDE :, :] = block.astype(BF16)


def unpack_member(in_ref, width):
    count = in_ref.shape[0]
    tiles = width // LANES
    main = [in_ref[:, q * WIDE : (q + 1) * WIDE, :].reshape(count * WIDE, LANES) for q in range(tiles)]
    main = jnp.concatenate(main, axis=1)
    room = (in_ref.shape[1] - tiles * WIDE) // 2
    block = in_ref[:, tiles * WIDE :, :].astype(F32)
    last = [unfold(block[:, s * room : s * room + tiles, :]) for s in range(2)]
    return main, jnp.concatenate(last, axis=0).astype(BF16)


def columns(rows):
    count = rows.shape[1]
    eye = (iota((count, count), 0) == iota((count, count), 1)).astype(F32)
    return dot(eye, rows.astype(F32), 1, 1)


def place(groups, tok_count, group_count):
    hit = groups[:, 0:1] == iota((tok_count, group_count), 1)
    for k in range(1, 3):
        hit = hit | (groups[:, k : k + 1] == iota((tok_count, group_count), 1))
    hit = hit.astype(F32)
    earlier = (iota((tok_count, tok_count), 1) < iota((tok_count, tok_count), 0)).astype(F32)
    position = jnp.where(hit > 0, dot(earlier, hit), 99.0)
    rows = group_count * SUB
    spread = (iota((rows, group_count), 0) >> 3 == iota((rows, group_count), 1)).astype(F32)
    at = dot(spread, position, 1, 1)
    main = (at == (iota((rows, tok_count), 0) & 7).astype(F32)).astype(F32)
    eye = (iota((group_count, group_count), 0) == iota((group_count, group_count), 1)).astype(F32)
    ninth = (dot(eye, position, 1, 1) == float(SUB)).astype(F32)
    return main, ninth, spread


def send_kernel(
    grad_hbm, groups_hbm, picks_hbm, gates_hbm, out_ref, grad_ref, groups_ref, picks_ref, gates_ref, sems,
    *, group_count,
):
    pairs = (
        (groups_hbm, groups_ref), (picks_hbm, picks_ref), (gates_hbm, gates_ref), (grad_hbm, grad_ref)
    )
    copies = [pltpu.make_async_copy(a, b, sems.at[i]) for i, (a, b) in enumerate(pairs)]
    for copy in copies:
        copy.start()
    for copy in copies[:3]:
        copy.wait()
    tok_count = grad_ref.shape[0]
    groups = columns(groups_ref[...]).astype(jnp.int32)
    picks = columns(picks_ref[...]).astype(jnp.int32)
    gates = columns(gates_ref[...])
    main, ninth, spread = place(groups, tok_count, group_count)
    table = jnp.zeros((tok_count, LANES), F32)
    for k in range(picks.shape[1]):
        pick = picks[:, k : k + 1]
        column = pick >> 3
        group = jnp.where(
            column == 0, groups[:, 0:1], jnp.where(column == 1, groups[:, 1:2], groups[:, 2:3])
        )
        expert = group * SUB + (pick & 7)
        table = table + jnp.where(expert == iota((tok_count, LANES), 1), gates[:, k : k + 1], 0.0)
    rows = group_count * SUB
    lane_of = iota((rows, LANES), 1)
    row_of = iota((rows, LANES), 0)
    same_within = ((iota((LANES, LANES), 0) & 7) == (iota((LANES, LANES), 1) & 7)).astype(F32)
    of_row = jnp.where(row_of >> 3 == lane_of >> 3, dot(main, table), 0.0)
    of_row = jnp.where((row_of & 7) == lane_of >> 3, dot(of_row, same_within), 0.0)
    extra = dot(spread, of_row, 0, 0)
    lane_of = iota((group_count, LANES), 1)
    of_row = jnp.where(iota((group_count, LANES), 0) == lane_of >> 3, dot(ninth, table), 0.0)
    extra = extra + jnp.where(lane_of >> 3 == SUB, dot(of_row, same_within), 0.0)
    copies[3].wait()
    grad = grad_ref[...]
    pack_group(out_ref, dot(main, grad), dot(ninth, grad), extra)


def route_kernel(in_ref, out_ref, main_ref, ninth_ref, *, width, cap):
    count, experts = in_ref.shape[0], SUB
    rows = count * SUB
    main, ninth, extra = unpack_group(in_ref, width)
    spread = (iota((count, rows), 1) >> 3 == iota((count, rows), 0)).astype(F32)
    wide = dot(extra, spread, 0, 0)
    wide = jnp.where(iota((LANES, rows), 0) >> 3 == (iota((LANES, rows), 1) & 7), wide, 0.0)
    pick = ((iota((experts, LANES), 1) & 7) == iota((experts, LANES), 0)).astype(F32)
    gate = dot(pick, wide)
    pick = (iota((experts, LANES), 1) == iota((experts, LANES), 0) + SUB * SUB).astype(F32)
    gate9 = dot(pick, extra, 1, 1)
    on, on9 = (gate > 0).astype(F32), (gate9 > 0).astype(F32)
    mm = (iota((rows, rows), 0) < iota((rows, rows), 1)).astype(F32)
    nm = (iota((count, rows), 0) < iota((count, rows), 1) >> 3).astype(F32)
    mn = (iota((rows, count), 0) >> 3 <= iota((rows, count), 1)).astype(F32)
    nn = (iota((count, count), 0) < iota((count, count), 1)).astype(F32)
    rank = dot(on, mm) + dot(on9, nm)
    rank9 = dot(on, mn) + dot(on9, nn)

    def weights(expert_of, slot_of):
        slots = expert_of.shape[0]
        expand = (expert_of[:, :experts] == iota((slots, experts), 1)).astype(F32)

        def one(rank, gate):
            slot = slot_of[:, : rank.shape[1]].astype(F32)
            value = dot(expand, gate)
            return jnp.where((dot(expand, rank) == slot) & (value > 0), value, 0.0)

        return one(rank, gate), one(rank9, gate9)

    big = iota((experts * WIDE, LANES), 0)
    small = iota((2 * experts, LANES), 0)
    weigh, weigh9 = weights(big >> 4, big & 15)
    last, last9 = weights(small & 7, WIDE + (small >> 3))
    first = dot(weigh, main) + dot(weigh9, ninth)
    second = dot(last, main) + dot(last9, ninth)
    pack_member(out_ref, first, second)
    main_ref[: experts * WIDE, :] = (weigh > 0).astype(F32).astype(BF16)
    main_ref[experts * WIDE :, :] = (last > 0).astype(F32).astype(BF16)
    ninth_ref[: experts * WIDE, :] = (weigh9 > 0).astype(F32).astype(BF16)
    ninth_ref[experts * WIDE :, :] = (last9 > 0).astype(F32).astype(BF16)


def prepare_kernel(flags_ref, *refs, cap):
    saved_hbm, gate_hbm, up_hbm, down_hbm = refs[:4]
    outs, scratch, sems = refs[-16:-11], refs[-11:-1], refs[-1]
    saved_ref, gate_ref, up_ref, down_ref, mine_ref, yours_ref, gate_t, up_t, down_t, _ = scratch

    @pl.when(flags_ref[0] == 1)
    def _():
        pairs = zip((saved_hbm, gate_hbm, up_hbm, down_hbm), (saved_ref, gate_ref, up_ref, down_ref))
        loads = [pltpu.make_async_copy(a, b, sems.at[i]) for i, (a, b) in enumerate(pairs)]
        results = (mine_ref, yours_ref, gate_t, up_t, down_t)
        stores = [
            pltpu.make_async_copy(a, b, sems.at[4 + i]) for i, (a, b) in enumerate(zip(results, outs))
        ]
        for load in loads:
            load.start()
        slots = saved_ref.shape[0]
        half = slots // 2
        experts = half // cap
        core = flags_ref[1]
        row = iota((slots, slots), 0)
        column = jnp.where(row < half, core, 1 - core)
        row = jnp.where(row < half, row, row - half)
        late = row - experts * WIDE
        member = jnp.where(late < 0, row >> 4, late & 7)
        place_in = jnp.where(late < 0, row & 15, WIDE + (late >> 3))
        order = iota((slots, slots), 1) == (2 * member + column) * cap + place_in
        loads[0].wait()
        rows = dot(order.astype(F32), saved_ref[...]).astype(BF16)
        loads[1].wait()
        pre_gate = dot(rows, gate_ref[...])
        loads[2].wait()
        pre_up = dot(rows, up_ref[...])
        gate = 1.0 / (1.0 + jnp.exp(-pre_gate))
        first = pre_up * gate * (1.0 + pre_gate * (1.0 - gate))
        factors = jnp.concatenate([first, pre_gate * gate], axis=1)
        mine_ref[...] = factors[:half]
        yours_ref[...] = factors[half:]
        stores[0].start()
        stores[1].start()
        gate_t[...] = gate_ref[...].T
        stores[2].start()
        up_t[...] = up_ref[...].T
        stores[3].start()
        loads[3].wait()
        down_t[...] = down_ref[...].T
        stores[4].start()
        for store in stores:
            store.wait()


def prepare(flags, inputs, earlier, cap):
    saved, gate, up, down = inputs
    slots, hidden = saved.shape[0], gate.shape[1]
    factor = jax.ShapeDtypeStruct((slots // 2, 2 * hidden), F32)
    outs = [factor, factor] + [
        jax.ShapeDtypeStruct(weight.shape[::-1], BF16) for weight in (gate, up, down)
    ]
    return pl.pallas_call(
        lambda *refs: prepare_kernel(*refs, cap=cap),
        out_shape=[pltpu.HBM(x.shape, x.dtype) for x in outs],
        in_specs=[pl.BlockSpec(memory_space=pltpu.SMEM)] + [HBM] * (4 + len(earlier)),
        out_specs=[HBM] * len(outs),
        scratch_shapes=[pltpu.VMEM(x.shape, x.dtype) for x in (*inputs, *outs)]
        + [pltpu.VMEM((SUB, LANES), F32), pltpu.SemaphoreType.DMA((9,))],
        input_output_aliases={5 + i: i for i in range(len(earlier))},
        cost_estimate=pl.CostEstimate(flops=6 * 10**9, bytes_accessed=20 * 10**6, transcendentals=0),
        compiler_params=pltpu.CompilerParams(vmem_limit_bytes=40 * 1024 * 1024),
    )(flags, *in_hbm(inputs), *in_hbm(earlier))


def expert_kernel(
    in_ref, factor_ref, factor2_ref, down_hbm, down2_hbm, gate_hbm, up_hbm, gate2_hbm, up2_hbm, out_ref,
    down_ref, down2_ref, gate_ref, up_ref, gate2_ref, up2_ref, sems,
):
    width, hidden = down_ref.shape
    sources = (down_hbm, down2_hbm, gate_hbm, up_hbm, gate2_hbm, up2_hbm)
    weights = (down_ref, down2_ref, gate_ref, up_ref, gate2_ref, up2_ref)
    copies = [
        pltpu.make_async_copy(source, weight, sems.at[i])
        for i, (source, weight) in enumerate(zip(sources, weights))
    ]
    for copy in copies:
        copy.start()
    main, last = unpack_member(in_ref, width)
    split = main.shape[0]
    rows = jnp.concatenate([main, last], axis=0)
    sides = []
    for i, factor in enumerate((factor_ref, factor2_ref)):
        copies[i].wait()
        grad = dot(rows, weights[i][...])
        sides.append((grad * factor[:, :hidden]).astype(BF16))
        sides.append((grad * factor[:, hidden:]).astype(BF16))
    for copy in copies[2:]:
        copy.wait()
    parts = dot(sides[0], gate_ref[...])
    for side, weight in zip(sides[1:], (up_ref, gate2_ref, up2_ref)):
        parts = parts + dot(side, weight[...])
    pack_member(out_ref, parts[:split], parts[split:])


def gather_kernel(in_ref, main_ref, ninth_ref, out_ref, *, width):
    main, last = unpack_member(in_ref, width)
    split = main.shape[0]
    total = dot(main_ref[:split, :], main, 0, 0) + dot(main_ref[split:, :], last, 0, 0)
    total9 = dot(ninth_ref[:split, :], main, 0, 0) + dot(ninth_ref[split:, :], last, 0, 0)
    pack_group(out_ref, total, total9, jnp.zeros((out_ref.shape[0], LANES), F32))


def place_kernel(groups_ref, main_ref, ninth_ref):
    groups = columns(groups_ref[...]).astype(jnp.int32)
    main, ninth, _ = place(groups, main_ref.shape[1], ninth_ref.shape[0])
    main_ref[...] = main.astype(BF16)
    ninth_ref[...] = ninth.astype(BF16)


def final_kernel(in_ref, main_ref, ninth_ref, out_ref):
    rows, rows9, _ = unpack_group(in_ref, out_ref.shape[1])
    total = dot(main_ref[...], rows, 0, 0) + dot(ninth_ref[...], rows9, 0, 0)
    out_ref[...] = total.astype(BF16)


HBM = pl.BlockSpec(memory_space=pltpu.HBM)
VMEM = pl.BlockSpec(memory_space=pltpu.VMEM)


def in_hbm(arrays):
    return [pltpu.with_memory_space_constraint(x, pltpu.HBM) for x in arrays]


def call(kernel, outs, *args):
    shapes = [jax.ShapeDtypeStruct(shape, BF16) for shape in outs]
    return pl.pallas_call(
        kernel,
        out_shape=shapes if len(shapes) > 1 else shapes[0],
        compiler_params=pltpu.CompilerParams(vmem_limit_bytes=32 * 1024 * 1024),
    )(*args)


def expert_parts(rows, *weights):
    factors, matrices = weights[:2], in_hbm(weights[2:])
    return pl.pallas_call(
        expert_kernel,
        out_shape=jax.ShapeDtypeStruct(rows.shape, BF16),
        in_specs=[VMEM] * 3 + [HBM] * 6,
        out_specs=VMEM,
        scratch_shapes=[pltpu.VMEM(weight.shape, BF16) for weight in matrices]
        + [pltpu.SemaphoreType.DMA((len(matrices),))],
        compiler_params=pltpu.CompilerParams(vmem_limit_bytes=40 * 1024 * 1024),
    )(rows, *factors, *matrices)


def body(out_grad, groups, picks, gates, w_gate, w_up, w_down, saved):
    group_count = lax.axis_size("group")
    member_count = lax.axis_size("member")
    experts = member_count // 2
    tok_count, width = out_grad.shape
    cap = 12 * tok_count // member_count
    slots = experts * cap
    same_core = [list(range(c, member_count, 2)) for c in range(2)]
    swap = [(i, i ^ 1) for i in range(member_count)]
    core = lax.axis_index("member") % 2
    group_shape = (group_count, width * SUB // LANES + 24, LANES)
    member_shape = (experts, width * WIDE // LANES + 48, LANES)

    def over_group(rows):
        return lax.all_to_all(rows, "group", split_axis=0, concat_axis=0, tiled=True)

    def over_member(rows):
        return lax.all_to_all(
            rows, "member", split_axis=0, concat_axis=0, axis_index_groups=same_core, tiled=True
        )

    def across(rows):
        return lax.ppermute(rows, "member", swap)

    def send(*args):
        return pl.pallas_call(
            lambda *refs: send_kernel(*refs, group_count=group_count),
            out_shape=jax.ShapeDtypeStruct(group_shape, BF16),
            in_specs=[HBM] * len(args),
            out_specs=VMEM,
            scratch_shapes=[pltpu.VMEM(arg.shape, arg.dtype) for arg in args]
            + [pltpu.SemaphoreType.DMA((len(args),))],
            compiler_params=pltpu.CompilerParams(vmem_limit_bytes=32 * 1024 * 1024),
        )(*in_hbm(args))

    w_gate, w_up, w_down, inputs = w_gate[0, 0], w_up[0, 0], w_down[0, 0], saved[0, 0]
    inputs = (inputs, w_gate, w_up, w_down)
    payload = send(out_grad, groups.T, picks.T, gates.T)
    payload, *inputs = lax.optimization_barrier((payload, *inputs))
    earlier = prepare(jnp.stack([1 - core, core]).astype(jnp.int32), inputs, (), cap)
    payload, *earlier = lax.optimization_barrier((payload, *earlier))
    arrived = over_group(payload)
    prepared = prepare(jnp.stack([core, core]).astype(jnp.int32), inputs, tuple(earlier), cap)
    mine, yours, w_gate, w_up, w_down = prepared
    yours, w_down2, w_gate2, w_up2 = [across(x) for x in (yours, w_down, w_gate, w_up)]

    def route(rows):
        kernel = lambda *refs: route_kernel(*refs, width=width, cap=cap)
        return call(
            kernel, [member_shape, (slots, group_count * SUB), (slots, group_count)], rows
        )

    scaled, routing, routing9 = route(arrived)
    weights = (mine, yours, w_down, w_down2, w_gate, w_up, w_gate2, w_up2)
    scaled, *weights = lax.optimization_barrier((scaled,) + weights)
    returned = over_member(expert_parts(over_member(scaled), *weights))
    sums = call(
        lambda *refs: gather_kernel(*refs, width=width),
        [group_shape],
        returned,
        routing,
        routing9,
    )
    sums, groups = lax.optimization_barrier((sums, groups.T))
    back = over_group(sums)
    placing = call(
        place_kernel, [(group_count * SUB, tok_count), (group_count, tok_count)], groups
    )
    return call(final_kernel, [(tok_count, width)], back, *placing)


def solution(mesh):
    token = P(("dp", "group", "member"), None)
    weight = P("group", "member", None, None)
    return jax.shard_map(
        body,
        mesh=mesh,
        in_specs=(token,) * 4 + (weight,) * 3 + (P("group", "member", "dp", None),),
        out_specs=token,
        check_vma=False,
    )
```

```python
import jax
import jax.numpy as jnp
from jax import lax
from jax.experimental import pallas as pl
from jax.experimental.pallas import tpu as pltpu
from jax.sharding import PartitionSpec as P

LANES = 128
SUB = 8
WIDE = 16
F32 = jnp.float32
BF16 = jnp.bfloat16


def iota(shape, dim):
    return lax.broadcasted_iota(jnp.int32, shape, dim)


def dot(a, b, left=1, right=0):
    return lax.dot_general(
        a.astype(BF16), b.astype(BF16), (((left,), (right,)), ((), ())), preferred_element_type=F32
    )


def fold(rows):
    return rows.reshape(rows.shape[0], rows.shape[1] // LANES, LANES)


def unfold(rows):
    return rows.reshape(rows.shape[0], rows.shape[1] * LANES)


def pack_group(out_ref, main, ninth, extra):
    count, width = ninth.shape
    half = width // 2
    main = main.reshape(count, SUB, width)
    tiles = half // LANES
    for q in range(tiles):
        low = main[:, :, q * LANES : (q + 1) * LANES]
        high = main[:, :, half + q * LANES : half + (q + 1) * LANES]
        tile = jnp.concatenate([low, high], axis=1)
        out_ref[:, q * WIDE : (q + 1) * WIDE, :] = tile.astype(BF16)
    tail = out_ref.shape[1] - tiles * WIDE
    pad = tail - width // LANES - 1
    block = jnp.concatenate(
        [fold(ninth), extra.reshape(count, 1, LANES), jnp.zeros((count, pad, LANES), F32)], axis=1
    )
    out_ref[:, tiles * WIDE :, :] = block.astype(BF16)


def unpack_group(in_ref, width):
    count = in_ref.shape[0]
    tiles = width // 2 // LANES
    low, high = [], []
    for q in range(tiles):
        tile = in_ref[:, q * WIDE : (q + 1) * WIDE, :].astype(F32)
        low.append(tile[:, :SUB, :].reshape(count * SUB, LANES).astype(BF16))
        high.append(tile[:, SUB:, :].reshape(count * SUB, LANES).astype(BF16))
    main = jnp.concatenate(low + high, axis=1)
    block = in_ref[:, tiles * WIDE :, :].astype(F32)
    ninth = unfold(block[:, : width // LANES, :])
    extra = block[:, width // LANES, :]
    return main, ninth.astype(BF16), extra


def pack_member(out_ref, main, last):
    count = out_ref.shape[0]
    width = main.shape[1]
    tiles = width // LANES
    main = main.astype(BF16).reshape(count, WIDE, width)
    for q in range(tiles):
        out_ref[:, q * WIDE : (q + 1) * WIDE, :] = main[:, :, q * LANES : (q + 1) * LANES]
    room = (out_ref.shape[1] - tiles * WIDE) // 2
    pad = jnp.zeros((count, room - tiles, LANES), F32)
    last = fold(last)
    block = jnp.concatenate([last[:count], pad, last[count:], pad], axis=1)
    out_ref[:, tiles * WIDE :, :] = block.astype(BF16)


def unpack_member(in_ref, width):
    count = in_ref.shape[0]
    tiles = width // LANES
    main = [in_ref[:, q * WIDE : (q + 1) * WIDE, :].reshape(count * WIDE, LANES) for q in range(tiles)]
    main = jnp.concatenate(main, axis=1)
    room = (in_ref.shape[1] - tiles * WIDE) // 2
    block = in_ref[:, tiles * WIDE :, :].astype(F32)
    last = [unfold(block[:, s * room : s * room + tiles, :]) for s in range(2)]
    return main, jnp.concatenate(last, axis=0).astype(BF16)


def columns(rows):
    count = rows.shape[1]
    eye = (iota((count, count), 0) == iota((count, count), 1)).astype(F32)
    return dot(eye, rows.astype(F32), 1, 1)


def place(groups, tok_count, group_count):
    hit = groups[:, 0:1] == iota((tok_count, group_count), 1)
    for k in range(1, 3):
        hit = hit | (groups[:, k : k + 1] == iota((tok_count, group_count), 1))
    hit = hit.astype(F32)
    earlier = (iota((tok_count, tok_count), 1) < iota((tok_count, tok_count), 0)).astype(F32)
    position = jnp.where(hit > 0, dot(earlier, hit), 99.0)
    rows = group_count * SUB
    spread = (iota((rows, group_count), 0) >> 3 == iota((rows, group_count), 1)).astype(F32)
    at = dot(spread, position, 1, 1)
    main = (at == (iota((rows, tok_count), 0) & 7).astype(F32)).astype(F32)
    eye = (iota((group_count, group_count), 0) == iota((group_count, group_count), 1)).astype(F32)
    ninth = (dot(eye, position, 1, 1) == float(SUB)).astype(F32)
    return main, ninth, spread


def send_kernel(
    grad_hbm, groups_hbm, picks_hbm, gates_hbm, out_ref, grad_ref, groups_ref, picks_ref, gates_ref, sems,
    *, group_count,
):
    pairs = (
        (groups_hbm, groups_ref), (picks_hbm, picks_ref), (gates_hbm, gates_ref), (grad_hbm, grad_ref)
    )
    copies = [pltpu.make_async_copy(a, b, sems.at[i]) for i, (a, b) in enumerate(pairs)]
    for copy in copies:
        copy.start()
    for copy in copies[:3]:
        copy.wait()
    tok_count = grad_ref.shape[0]
    groups = columns(groups_ref[...]).astype(jnp.int32)
    picks = columns(picks_ref[...]).astype(jnp.int32)
    gates = columns(gates_ref[...])
    main, ninth, spread = place(groups, tok_count, group_count)
    table = jnp.zeros((tok_count, LANES), F32)
    for k in range(picks.shape[1]):
        pick = picks[:, k : k + 1]
        column = pick >> 3
        group = jnp.where(
            column == 0, groups[:, 0:1], jnp.where(column == 1, groups[:, 1:2], groups[:, 2:3])
        )
        expert = group * SUB + (pick & 7)
        table = table + jnp.where(expert == iota((tok_count, LANES), 1), gates[:, k : k + 1], 0.0)
    rows = group_count * SUB
    lane_of = iota((rows, LANES), 1)
    row_of = iota((rows, LANES), 0)
    same_within = ((iota((LANES, LANES), 0) & 7) == (iota((LANES, LANES), 1) & 7)).astype(F32)
    of_row = jnp.where(row_of >> 3 == lane_of >> 3, dot(main, table), 0.0)
    of_row = jnp.where((row_of & 7) == lane_of >> 3, dot(of_row, same_within), 0.0)
    extra = dot(spread, of_row, 0, 0)
    lane_of = iota((group_count, LANES), 1)
    of_row = jnp.where(iota((group_count, LANES), 0) == lane_of >> 3, dot(ninth, table), 0.0)
    extra = extra + jnp.where(lane_of >> 3 == SUB, dot(of_row, same_within), 0.0)
    copies[3].wait()
    grad = grad_ref[...]
    pack_group(out_ref, dot(main, grad), dot(ninth, grad), extra)


def route_kernel(in_ref, out_ref, main_ref, ninth_ref, *, width, cap):
    count, experts = in_ref.shape[0], SUB
    rows = count * SUB
    main, ninth, extra = unpack_group(in_ref, width)
    spread = (iota((count, rows), 1) >> 3 == iota((count, rows), 0)).astype(F32)
    wide = dot(extra, spread, 0, 0)
    wide = jnp.where(iota((LANES, rows), 0) >> 3 == (iota((LANES, rows), 1) & 7), wide, 0.0)
    pick = ((iota((experts, LANES), 1) & 7) == iota((experts, LANES), 0)).astype(F32)
    gate = dot(pick, wide)
    pick = (iota((experts, LANES), 1) == iota((experts, LANES), 0) + SUB * SUB).astype(F32)
    gate9 = dot(pick, extra, 1, 1)
    on, on9 = (gate > 0).astype(F32), (gate9 > 0).astype(F32)
    mm = (iota((rows, rows), 0) < iota((rows, rows), 1)).astype(F32)
    nm = (iota((count, rows), 0) < iota((count, rows), 1) >> 3).astype(F32)
    mn = (iota((rows, count), 0) >> 3 <= iota((rows, count), 1)).astype(F32)
    nn = (iota((count, count), 0) < iota((count, count), 1)).astype(F32)
    rank = dot(on, mm) + dot(on9, nm)
    rank9 = dot(on, mn) + dot(on9, nn)

    def weights(expert_of, slot_of):
        slots = expert_of.shape[0]
        expand = (expert_of[:, :experts] == iota((slots, experts), 1)).astype(F32)

        def one(rank, gate):
            slot = slot_of[:, : rank.shape[1]].astype(F32)
            value = dot(expand, gate)
            return jnp.where((dot(expand, rank) == slot) & (value > 0), value, 0.0)

        return one(rank, gate), one(rank9, gate9)

    big = iota((experts * WIDE, LANES), 0)
    small = iota((2 * experts, LANES), 0)
    weigh, weigh9 = weights(big >> 4, big & 15)
    last, last9 = weights(small & 7, WIDE + (small >> 3))
    first = dot(weigh, main) + dot(weigh9, ninth)
    second = dot(last, main) + dot(last9, ninth)
    pack_member(out_ref, first, second)
    main_ref[: experts * WIDE, :] = (weigh > 0).astype(F32).astype(BF16)
    main_ref[experts * WIDE :, :] = (last > 0).astype(F32).astype(BF16)
    ninth_ref[: experts * WIDE, :] = (weigh9 > 0).astype(F32).astype(BF16)
    ninth_ref[experts * WIDE :, :] = (last9 > 0).astype(F32).astype(BF16)


def prepare_kernel(flags_ref, *refs, cap):
    saved_hbm, gate_hbm, up_hbm, down_hbm = refs[:4]
    mine_hbm, yours_hbm, gate_t, up_t, down_t = refs[-12:-7]
    saved_ref, tall_ref, wide_ref, mine_ref, yours_ref, factor_sems, sems = refs[-7:]

    @pl.when(flags_ref[0] == 1)
    def _():
        def load(source, target):
            return pltpu.make_async_copy(source, target, sems.at[0])

        def store(source, target):
            return pltpu.make_async_copy(source, target, sems.at[1])

        first_load = pltpu.make_async_copy(saved_hbm, saved_ref, factor_sems.at[0])
        first_load.start()
        gate_load, up_load = load(gate_hbm, tall_ref), load(up_hbm, tall_ref)
        down_load = load(down_hbm, wide_ref)
        gate_load.start()
        slots = saved_ref.shape[0]
        half = slots // 2
        experts = half // cap
        core = flags_ref[1]
        row = iota((slots, slots), 0)
        column = jnp.where(row < half, core, 1 - core)
        row = jnp.where(row < half, row, row - half)
        late = row - experts * WIDE
        member = jnp.where(late < 0, row >> 4, late & 7)
        place_in = jnp.where(late < 0, row & 15, WIDE + (late >> 3))
        order = iota((slots, slots), 1) == (2 * member + column) * cap + place_in
        first_load.wait()
        rows = dot(order.astype(F32), saved_ref[...]).astype(BF16)
        gate_load.wait()
        pre_gate = dot(rows, tall_ref[...])
        wide_ref[...] = tall_ref[...].T
        gate_store = store(wide_ref, gate_t)
        gate_store.start()
        up_load.start()
        up_load.wait()
        pre_up = dot(rows, tall_ref[...])
        gate = 1.0 / (1.0 + jnp.exp(-pre_gate))
        first = pre_up * gate * (1.0 + pre_gate * (1.0 - gate))
        factors = jnp.concatenate([first, pre_gate * gate], axis=1)
        mine_ref[...] = factors[:half]
        yours_ref[...] = factors[half:]
        stores = [
            pltpu.make_async_copy(mine_ref, mine_hbm, factor_sems.at[1]),
            pltpu.make_async_copy(yours_ref, yours_hbm, factor_sems.at[2]),
        ]
        for one in stores:
            one.start()
        gate_store.wait()
        wide_ref[...] = tall_ref[...].T
        up_store = store(wide_ref, up_t)
        up_store.start()
        up_store.wait()
        down_load.start()
        down_load.wait()
        tall_ref[...] = wide_ref[...].T
        down_store = store(tall_ref, down_t)
        down_store.start()
        down_store.wait()
        for one in stores:
            one.wait()


def prepare(flags, inputs, earlier, cap):
    saved, gate, up, down = inputs
    slots, hidden = saved.shape[0], gate.shape[1]
    factor = jax.ShapeDtypeStruct((slots // 2, 2 * hidden), F32)
    outs = [factor, factor] + [
        jax.ShapeDtypeStruct(weight.shape[::-1], BF16) for weight in (gate, up, down)
    ]
    return pl.pallas_call(
        lambda *refs: prepare_kernel(*refs, cap=cap),
        out_shape=[pltpu.HBM(x.shape, x.dtype) for x in outs],
        in_specs=[pl.BlockSpec(memory_space=pltpu.SMEM)] + [HBM] * (4 + len(earlier)),
        out_specs=[HBM] * len(outs),
        scratch_shapes=[pltpu.VMEM(x.shape, x.dtype) for x in (saved, gate, down, factor, factor)]
        + [pltpu.SemaphoreType.DMA((3,)), pltpu.SemaphoreType.DMA((2,))],
        input_output_aliases={5 + i: i for i in range(len(earlier))},
        cost_estimate=pl.CostEstimate(flops=6 * 10**9, bytes_accessed=20 * 10**6, transcendentals=0),
        compiler_params=pltpu.CompilerParams(vmem_limit_bytes=40 * 1024 * 1024),
    )(flags, *in_hbm(inputs), *in_hbm(earlier))


def expert_kernel(
    in_ref, factor_ref, factor2_ref, down_hbm, down2_hbm, gate_hbm, up_hbm, gate2_hbm, up2_hbm, out_ref,
    down_ref, down2_ref, gate_ref, up_ref, gate2_ref, up2_ref, sems,
):
    width, hidden = down_ref.shape
    sources = (down_hbm, down2_hbm, gate_hbm, up_hbm, gate2_hbm, up2_hbm)
    weights = (down_ref, down2_ref, gate_ref, up_ref, gate2_ref, up2_ref)
    copies = [
        pltpu.make_async_copy(source, weight, sems.at[i])
        for i, (source, weight) in enumerate(zip(sources, weights))
    ]
    for copy in copies:
        copy.start()
    main, last = unpack_member(in_ref, width)
    split = main.shape[0]
    rows = jnp.concatenate([main, last], axis=0)
    sides = []
    for i, factor in enumerate((factor_ref, factor2_ref)):
        copies[i].wait()
        grad = dot(rows, weights[i][...])
        sides.append((grad * factor[:, :hidden]).astype(BF16))
        sides.append((grad * factor[:, hidden:]).astype(BF16))
    copies[2].wait()
    parts = dot(sides[0], gate_ref[...])
    for side, weight, copy in zip(sides[1:], (up_ref, gate2_ref, up2_ref), copies[3:]):
        copy.wait()
        parts = parts + dot(side, weight[...])
    pack_member(out_ref, parts[:split], parts[split:])


def gather_kernel(in_ref, main_ref, ninth_ref, out_ref, *, width):
    main, last = unpack_member(in_ref, width)
    split = main.shape[0]
    total = dot(main_ref[:split, :], main, 0, 0) + dot(main_ref[split:, :], last, 0, 0)
    total9 = dot(ninth_ref[:split, :], main, 0, 0) + dot(ninth_ref[split:, :], last, 0, 0)
    pack_group(out_ref, total, total9, jnp.zeros((out_ref.shape[0], LANES), F32))


def place_kernel(groups_ref, main_ref, ninth_ref):
    groups = columns(groups_ref[...]).astype(jnp.int32)
    main, ninth, _ = place(groups, main_ref.shape[1], ninth_ref.shape[0])
    main_ref[...] = main.astype(BF16)
    ninth_ref[...] = ninth.astype(BF16)


def final_kernel(in_ref, main_ref, ninth_ref, out_ref):
    rows, rows9, _ = unpack_group(in_ref, out_ref.shape[1])
    total = dot(main_ref[...], rows, 0, 0) + dot(ninth_ref[...], rows9, 0, 0)
    out_ref[...] = total.astype(BF16)


HBM = pl.BlockSpec(memory_space=pltpu.HBM)
VMEM = pl.BlockSpec(memory_space=pltpu.VMEM)


def in_hbm(arrays):
    return [pltpu.with_memory_space_constraint(x, pltpu.HBM) for x in arrays]


def call(kernel, outs, *args):
    shapes = [jax.ShapeDtypeStruct(shape, BF16) for shape in outs]
    return pl.pallas_call(
        kernel,
        out_shape=shapes if len(shapes) > 1 else shapes[0],
        compiler_params=pltpu.CompilerParams(vmem_limit_bytes=32 * 1024 * 1024),
    )(*args)


def expert_parts(rows, *weights):
    factors, matrices = weights[:2], in_hbm(weights[2:])
    return pl.pallas_call(
        expert_kernel,
        out_shape=jax.ShapeDtypeStruct(rows.shape, BF16),
        in_specs=[VMEM] * 3 + [HBM] * 6,
        out_specs=VMEM,
        scratch_shapes=[pltpu.VMEM(weight.shape, BF16) for weight in matrices]
        + [pltpu.SemaphoreType.DMA((len(matrices),))],
        compiler_params=pltpu.CompilerParams(vmem_limit_bytes=40 * 1024 * 1024),
    )(rows, *factors, *matrices)


def body(out_grad, groups, picks, gates, w_gate, w_up, w_down, saved):
    group_count = lax.axis_size("group")
    member_count = lax.axis_size("member")
    experts = member_count // 2
    tok_count, width = out_grad.shape
    cap = 12 * tok_count // member_count
    slots = experts * cap
    same_core = [list(range(c, member_count, 2)) for c in range(2)]
    swap = [(i, i ^ 1) for i in range(member_count)]
    core = lax.axis_index("member") % 2
    group_shape = (group_count, width * SUB // LANES + 24, LANES)
    member_shape = (experts, width * WIDE // LANES + 48, LANES)

    def over_group(rows):
        return lax.all_to_all(rows, "group", split_axis=0, concat_axis=0, tiled=True)

    def over_member(rows):
        return lax.all_to_all(
            rows, "member", split_axis=0, concat_axis=0, axis_index_groups=same_core, tiled=True
        )

    def across(rows):
        return lax.ppermute(rows, "member", swap)

    def send(*args):
        return pl.pallas_call(
            lambda *refs: send_kernel(*refs, group_count=group_count),
            out_shape=jax.ShapeDtypeStruct(group_shape, BF16),
            in_specs=[HBM] * len(args),
            out_specs=VMEM,
            scratch_shapes=[pltpu.VMEM(arg.shape, arg.dtype) for arg in args]
            + [pltpu.SemaphoreType.DMA((len(args),))],
            compiler_params=pltpu.CompilerParams(vmem_limit_bytes=32 * 1024 * 1024),
        )(*in_hbm(args))

    w_gate, w_up, w_down, inputs = w_gate[0, 0], w_up[0, 0], w_down[0, 0], saved[0, 0]
    inputs = (inputs, w_gate, w_up, w_down)
    payload = send(out_grad, groups.T, picks.T, gates.T)
    payload, *inputs = lax.optimization_barrier((payload, *inputs))
    earlier = prepare(jnp.stack([1 - core, core]).astype(jnp.int32), inputs, (), cap)
    payload, *earlier = lax.optimization_barrier((payload, *earlier))
    arrived = over_group(payload)
    prepared = prepare(jnp.stack([core, core]).astype(jnp.int32), inputs, tuple(earlier), cap)
    mine, yours, w_gate, w_up, w_down = prepared
    yours, w_down2, w_gate2, w_up2 = [across(x) for x in (yours, w_down, w_gate, w_up)]

    def route(rows):
        kernel = lambda *refs: route_kernel(*refs, width=width, cap=cap)
        return call(
            kernel, [member_shape, (slots, group_count * SUB), (slots, group_count)], rows
        )

    scaled, routing, routing9 = route(arrived)
    weights = (mine, yours, w_down, w_down2, w_gate, w_up, w_gate2, w_up2)
    scaled, *weights = lax.optimization_barrier((scaled,) + weights)
    returned = over_member(expert_parts(over_member(scaled), *weights))
    sums = call(
        lambda *refs: gather_kernel(*refs, width=width),
        [group_shape],
        returned,
        routing,
        routing9,
    )
    sums, groups = lax.optimization_barrier((sums, groups.T))
    back = over_group(sums)
    placing = call(
        place_kernel, [(group_count * SUB, tok_count), (group_count, tok_count)], groups
    )
    return call(final_kernel, [(tok_count, width)], back, *placing)


def solution(mesh):
    token = P(("dp", "group", "member"), None)
    weight = P("group", "member", None, None)
    return jax.shard_map(
        body,
        mesh=mesh,
        in_specs=(token,) * 4 + (weight,) * 3 + (P("group", "member", "dp", None),),
        out_specs=token,
        check_vma=False,
    )
```

```python
import jax
import jax.numpy as jnp
from jax import lax
from jax.experimental import pallas as pl
from jax.experimental.pallas import tpu as pltpu
from jax.sharding import PartitionSpec as P

LANES = 128
SUB = 8
WIDE = 16
F32 = jnp.float32
BF16 = jnp.bfloat16


def iota(shape, dim):
    return lax.broadcasted_iota(jnp.int32, shape, dim)


def dot(a, b, left=1, right=0):
    return lax.dot_general(
        a.astype(BF16), b.astype(BF16), (((left,), (right,)), ((), ())), preferred_element_type=F32
    )


def fold(rows):
    return rows.reshape(rows.shape[0], rows.shape[1] // LANES, LANES)


def unfold(rows):
    return rows.reshape(rows.shape[0], rows.shape[1] * LANES)


def pack_group(out_ref, main, ninth, extra):
    count, width = ninth.shape
    half = width // 2
    main = main.reshape(count, SUB, width)
    tiles = half // LANES
    for q in range(tiles):
        low = main[:, :, q * LANES : (q + 1) * LANES]
        high = main[:, :, half + q * LANES : half + (q + 1) * LANES]
        tile = jnp.concatenate([low, high], axis=1)
        out_ref[:, q * WIDE : (q + 1) * WIDE, :] = tile.astype(BF16)
    tail = out_ref.shape[1] - tiles * WIDE
    pad = tail - width // LANES - 1
    block = jnp.concatenate(
        [fold(ninth), extra.reshape(count, 1, LANES), jnp.zeros((count, pad, LANES), F32)], axis=1
    )
    out_ref[:, tiles * WIDE :, :] = block.astype(BF16)


def unpack_group(in_ref, width):
    count = in_ref.shape[0]
    tiles = width // 2 // LANES
    low, high = [], []
    for q in range(tiles):
        tile = in_ref[:, q * WIDE : (q + 1) * WIDE, :].astype(F32)
        low.append(tile[:, :SUB, :].reshape(count * SUB, LANES).astype(BF16))
        high.append(tile[:, SUB:, :].reshape(count * SUB, LANES).astype(BF16))
    main = jnp.concatenate(low + high, axis=1)
    block = in_ref[:, tiles * WIDE :, :].astype(F32)
    ninth = unfold(block[:, : width // LANES, :])
    extra = block[:, width // LANES, :]
    return main, ninth.astype(BF16), extra


def pack_member(out_ref, main, last):
    count = out_ref.shape[0]
    width = main.shape[1]
    tiles = width // LANES
    main = main.astype(BF16).reshape(count, WIDE, width)
    for q in range(tiles):
        out_ref[:, q * WIDE : (q + 1) * WIDE, :] = main[:, :, q * LANES : (q + 1) * LANES]
    room = (out_ref.shape[1] - tiles * WIDE) // 2
    pad = jnp.zeros((count, room - tiles, LANES), F32)
    last = fold(last)
    block = jnp.concatenate([last[:count], pad, last[count:], pad], axis=1)
    out_ref[:, tiles * WIDE :, :] = block.astype(BF16)


def unpack_member(in_ref, width):
    count = in_ref.shape[0]
    tiles = width // LANES
    main = [in_ref[:, q * WIDE : (q + 1) * WIDE, :].reshape(count * WIDE, LANES) for q in range(tiles)]
    main = jnp.concatenate(main, axis=1)
    room = (in_ref.shape[1] - tiles * WIDE) // 2
    block = in_ref[:, tiles * WIDE :, :].astype(F32)
    last = [unfold(block[:, s * room : s * room + tiles, :]) for s in range(2)]
    return main, jnp.concatenate(last, axis=0).astype(BF16)


def columns(rows):
    count = rows.shape[1]
    eye = (iota((count, count), 0) == iota((count, count), 1)).astype(F32)
    return dot(eye, rows.astype(F32), 1, 1)


def place(groups, tok_count, group_count):
    hit = groups[:, 0:1] == iota((tok_count, group_count), 1)
    for k in range(1, 3):
        hit = hit | (groups[:, k : k + 1] == iota((tok_count, group_count), 1))
    hit = hit.astype(F32)
    earlier = (iota((tok_count, tok_count), 1) < iota((tok_count, tok_count), 0)).astype(F32)
    position = jnp.where(hit > 0, dot(earlier, hit), 99.0)
    rows = group_count * SUB
    spread = (iota((rows, group_count), 0) >> 3 == iota((rows, group_count), 1)).astype(F32)
    at = dot(spread, position, 1, 1)
    main = (at == (iota((rows, tok_count), 0) & 7).astype(F32)).astype(F32)
    eye = (iota((group_count, group_count), 0) == iota((group_count, group_count), 1)).astype(F32)
    ninth = (dot(eye, position, 1, 1) == float(SUB)).astype(F32)
    return main, ninth, spread


def send_kernel(
    grad_hbm, groups_hbm, picks_hbm, gates_hbm, out_ref, grad_ref, groups_ref, picks_ref, gates_ref, sems,
    *, group_count,
):
    pairs = (
        (groups_hbm, groups_ref), (picks_hbm, picks_ref), (gates_hbm, gates_ref), (grad_hbm, grad_ref)
    )
    copies = [pltpu.make_async_copy(a, b, sems.at[i]) for i, (a, b) in enumerate(pairs)]
    for copy in copies:
        copy.start()
    for copy in copies[:3]:
        copy.wait()
    tok_count = grad_ref.shape[0]
    groups = columns(groups_ref[...]).astype(jnp.int32)
    picks = columns(picks_ref[...]).astype(jnp.int32)
    gates = columns(gates_ref[...])
    main, ninth, spread = place(groups, tok_count, group_count)
    table = jnp.zeros((tok_count, LANES), F32)
    for k in range(picks.shape[1]):
        pick = picks[:, k : k + 1]
        column = pick >> 3
        group = jnp.where(
            column == 0, groups[:, 0:1], jnp.where(column == 1, groups[:, 1:2], groups[:, 2:3])
        )
        expert = group * SUB + (pick & 7)
        table = table + jnp.where(expert == iota((tok_count, LANES), 1), gates[:, k : k + 1], 0.0)
    rows = group_count * SUB
    lane_of = iota((rows, LANES), 1)
    row_of = iota((rows, LANES), 0)
    same_within = ((iota((LANES, LANES), 0) & 7) == (iota((LANES, LANES), 1) & 7)).astype(F32)
    of_row = jnp.where(row_of >> 3 == lane_of >> 3, dot(main, table), 0.0)
    of_row = jnp.where((row_of & 7) == lane_of >> 3, dot(of_row, same_within), 0.0)
    extra = dot(spread, of_row, 0, 0)
    lane_of = iota((group_count, LANES), 1)
    of_row = jnp.where(iota((group_count, LANES), 0) == lane_of >> 3, dot(ninth, table), 0.0)
    extra = extra + jnp.where(lane_of >> 3 == SUB, dot(of_row, same_within), 0.0)
    copies[3].wait()
    grad = grad_ref[...]
    pack_group(out_ref, dot(main, grad), dot(ninth, grad), extra)


def route_kernel(in_ref, out_ref, main_ref, ninth_ref, *, width, cap):
    count, experts = in_ref.shape[0], SUB
    rows = count * SUB
    main, ninth, extra = unpack_group(in_ref, width)
    spread = (iota((count, rows), 1) >> 3 == iota((count, rows), 0)).astype(F32)
    wide = dot(extra, spread, 0, 0)
    wide = jnp.where(iota((LANES, rows), 0) >> 3 == (iota((LANES, rows), 1) & 7), wide, 0.0)
    pick = ((iota((experts, LANES), 1) & 7) == iota((experts, LANES), 0)).astype(F32)
    gate = dot(pick, wide)
    pick = (iota((experts, LANES), 1) == iota((experts, LANES), 0) + SUB * SUB).astype(F32)
    gate9 = dot(pick, extra, 1, 1)
    on, on9 = (gate > 0).astype(F32), (gate9 > 0).astype(F32)
    mm = (iota((rows, rows), 0) < iota((rows, rows), 1)).astype(F32)
    nm = (iota((count, rows), 0) < iota((count, rows), 1) >> 3).astype(F32)
    mn = (iota((rows, count), 0) >> 3 <= iota((rows, count), 1)).astype(F32)
    nn = (iota((count, count), 0) < iota((count, count), 1)).astype(F32)
    rank = dot(on, mm) + dot(on9, nm)
    rank9 = dot(on, mn) + dot(on9, nn)

    def weights(expert_of, slot_of):
        slots = expert_of.shape[0]
        expand = (expert_of[:, :experts] == iota((slots, experts), 1)).astype(F32)

        def one(rank, gate):
            slot = slot_of[:, : rank.shape[1]].astype(F32)
            value = dot(expand, gate)
            return jnp.where((dot(expand, rank) == slot) & (value > 0), value, 0.0)

        return one(rank, gate), one(rank9, gate9)

    big = iota((experts * WIDE, LANES), 0)
    small = iota((2 * experts, LANES), 0)
    weigh, weigh9 = weights(big >> 4, big & 15)
    last, last9 = weights(small & 7, WIDE + (small >> 3))
    first = dot(weigh, main) + dot(weigh9, ninth)
    second = dot(last, main) + dot(last9, ninth)
    pack_member(out_ref, first, second)
    main_ref[: experts * WIDE, :] = (weigh > 0).astype(F32).astype(BF16)
    main_ref[experts * WIDE :, :] = (last > 0).astype(F32).astype(BF16)
    ninth_ref[: experts * WIDE, :] = (weigh9 > 0).astype(F32).astype(BF16)
    ninth_ref[experts * WIDE :, :] = (last9 > 0).astype(F32).astype(BF16)


def prepare_kernel(flags_ref, *refs, cap):
    saved_hbm, gate_hbm, up_hbm, down_hbm = refs[:4]
    mine_hbm, yours_hbm, gate_t, up_t, down_t = refs[-12:-7]
    saved_ref, tall_ref, wide_ref, mine_ref, yours_ref, factor_sems, sems = refs[-7:]

    @pl.when(flags_ref[0] == 1)
    def _():
        def load(source, target):
            return pltpu.make_async_copy(source, target, sems.at[0])

        def store(source, target):
            return pltpu.make_async_copy(source, target, sems.at[1])

        first_load = pltpu.make_async_copy(saved_hbm, saved_ref, factor_sems.at[0])
        first_load.start()
        gate_load, up_load = load(gate_hbm, tall_ref), load(up_hbm, tall_ref)
        down_load = load(down_hbm, wide_ref)
        gate_load.start()
        slots = saved_ref.shape[0]
        half = slots // 2
        experts = half // cap
        core = flags_ref[1]
        row = iota((slots, slots), 0)
        column = jnp.where(row < half, core, 1 - core)
        row = jnp.where(row < half, row, row - half)
        late = row - experts * WIDE
        member = jnp.where(late < 0, row >> 4, late & 7)
        place_in = jnp.where(late < 0, row & 15, WIDE + (late >> 3))
        order = iota((slots, slots), 1) == (2 * member + column) * cap + place_in
        first_load.wait()
        rows = dot(order.astype(F32), saved_ref[...]).astype(BF16)
        gate_load.wait()
        pre_gate = dot(rows, tall_ref[...])
        wide_ref[...] = tall_ref[...].T
        gate_store = store(wide_ref, gate_t)
        gate_store.start()
        up_load.start()
        up_load.wait()
        pre_up = dot(rows, tall_ref[...])
        gate = 1.0 / (1.0 + jnp.exp(-pre_gate))
        first = pre_up * gate * (1.0 + pre_gate * (1.0 - gate))
        factors = jnp.concatenate([first, pre_gate * gate], axis=1)
        mine_ref[...] = factors[:half]
        yours_ref[...] = factors[half:]
        stores = [
            pltpu.make_async_copy(mine_ref, mine_hbm, factor_sems.at[1]),
            pltpu.make_async_copy(yours_ref, yours_hbm, factor_sems.at[2]),
        ]
        for one in stores:
            one.start()
        gate_store.wait()
        wide_ref[...] = tall_ref[...].T
        up_store = store(wide_ref, up_t)
        up_store.start()
        up_store.wait()
        down_load.start()
        down_load.wait()
        tall_ref[...] = wide_ref[...].T
        down_store = store(tall_ref, down_t)
        down_store.start()
        down_store.wait()
        for one in stores:
            one.wait()


def prepared_shapes(saved, gate, up, down):
    slots, hidden = saved.shape[0], gate.shape[1]
    factor = jax.ShapeDtypeStruct((slots // 2, 2 * hidden), F32)
    outs = [factor, factor] + [
        jax.ShapeDtypeStruct(weight.shape[::-1], BF16) for weight in (gate, up, down)
    ]
    scratch = [pltpu.VMEM(x.shape, x.dtype) for x in (saved, gate, down, factor, factor)]
    return [pltpu.HBM(x.shape, x.dtype) for x in outs], scratch + [
        pltpu.SemaphoreType.DMA((3,)),
        pltpu.SemaphoreType.DMA((2,)),
    ]


def send(flags, rows, inputs, group_shape, cap):
    outs, scratch = prepared_shapes(*inputs)

    def kernel(flags_ref, *refs):
        send_kernel(*refs[:4], refs[8], *refs[14:19], group_count=group_shape[0])
        prepare_kernel(flags_ref, *refs[4:8], *refs[9:14], *refs[19:], cap=cap)

    return pl.pallas_call(
        kernel,
        out_shape=[jax.ShapeDtypeStruct(group_shape, BF16)] + outs,
        in_specs=[pl.BlockSpec(memory_space=pltpu.SMEM)] + [HBM] * 8,
        out_specs=[VMEM] + [HBM] * len(outs),
        scratch_shapes=[pltpu.VMEM(x.shape, x.dtype) for x in rows]
        + [pltpu.SemaphoreType.DMA((4,))]
        + scratch,
        compiler_params=pltpu.CompilerParams(vmem_limit_bytes=40 * 1024 * 1024),
    )(flags, *in_hbm(rows), *in_hbm(inputs))


def prepare(flags, inputs, earlier, cap):
    outs, scratch = prepared_shapes(*inputs)
    return pl.pallas_call(
        lambda *refs: prepare_kernel(*refs, cap=cap),
        out_shape=outs,
        in_specs=[pl.BlockSpec(memory_space=pltpu.SMEM)] + [HBM] * (4 + len(earlier)),
        out_specs=[HBM] * len(outs),
        scratch_shapes=scratch,
        input_output_aliases={5 + i: i for i in range(len(earlier))},
        cost_estimate=pl.CostEstimate(flops=6 * 10**9, bytes_accessed=20 * 10**6, transcendentals=0),
        compiler_params=pltpu.CompilerParams(vmem_limit_bytes=40 * 1024 * 1024),
    )(flags, *in_hbm(inputs), *in_hbm(earlier))


def expert_kernel(
    in_ref, factor_ref, factor2_ref, down_hbm, down2_hbm, gate_hbm, up_hbm, gate2_hbm, up2_hbm, out_ref,
    down_ref, down2_ref, gate_ref, up_ref, gate2_ref, up2_ref, sems,
):
    width, hidden = down_ref.shape
    sources = (down_hbm, down2_hbm, gate_hbm, up_hbm, gate2_hbm, up2_hbm)
    weights = (down_ref, down2_ref, gate_ref, up_ref, gate2_ref, up2_ref)
    copies = [
        pltpu.make_async_copy(source, weight, sems.at[i])
        for i, (source, weight) in enumerate(zip(sources, weights))
    ]
    for copy in copies:
        copy.start()
    main, last = unpack_member(in_ref, width)
    split = main.shape[0]
    rows = jnp.concatenate([main, last], axis=0)
    sides = []
    for i, factor in enumerate((factor_ref, factor2_ref)):
        copies[i].wait()
        grad = dot(rows, weights[i][...])
        sides.append((grad * factor[:, :hidden]).astype(BF16))
        sides.append((grad * factor[:, hidden:]).astype(BF16))
    copies[2].wait()
    parts = dot(sides[0], gate_ref[...])
    for side, weight, copy in zip(sides[1:], (up_ref, gate2_ref, up2_ref), copies[3:]):
        copy.wait()
        parts = parts + dot(side, weight[...])
    pack_member(out_ref, parts[:split], parts[split:])


def gather_kernel(in_ref, main_ref, ninth_ref, out_ref, *, width):
    main, last = unpack_member(in_ref, width)
    split = main.shape[0]
    total = dot(main_ref[:split, :], main, 0, 0) + dot(main_ref[split:, :], last, 0, 0)
    total9 = dot(ninth_ref[:split, :], main, 0, 0) + dot(ninth_ref[split:, :], last, 0, 0)
    pack_group(out_ref, total, total9, jnp.zeros((out_ref.shape[0], LANES), F32))


def place_kernel(groups_ref, main_ref, ninth_ref):
    groups = columns(groups_ref[...]).astype(jnp.int32)
    main, ninth, _ = place(groups, main_ref.shape[1], ninth_ref.shape[0])
    main_ref[...] = main.astype(BF16)
    ninth_ref[...] = ninth.astype(BF16)


def final_kernel(in_ref, main_ref, ninth_ref, out_ref):
    rows, rows9, _ = unpack_group(in_ref, out_ref.shape[1])
    total = dot(main_ref[...], rows, 0, 0) + dot(ninth_ref[...], rows9, 0, 0)
    out_ref[...] = total.astype(BF16)


HBM = pl.BlockSpec(memory_space=pltpu.HBM)
VMEM = pl.BlockSpec(memory_space=pltpu.VMEM)


def in_hbm(arrays):
    return [pltpu.with_memory_space_constraint(x, pltpu.HBM) for x in arrays]


def call(kernel, outs, *args):
    shapes = [jax.ShapeDtypeStruct(shape, BF16) for shape in outs]
    return pl.pallas_call(
        kernel,
        out_shape=shapes if len(shapes) > 1 else shapes[0],
        compiler_params=pltpu.CompilerParams(vmem_limit_bytes=32 * 1024 * 1024),
    )(*args)


def expert_parts(rows, *weights):
    factors, matrices = weights[:2], in_hbm(weights[2:])
    return pl.pallas_call(
        expert_kernel,
        out_shape=jax.ShapeDtypeStruct(rows.shape, BF16),
        in_specs=[VMEM] * 3 + [HBM] * 6,
        out_specs=VMEM,
        scratch_shapes=[pltpu.VMEM(weight.shape, BF16) for weight in matrices]
        + [pltpu.SemaphoreType.DMA((len(matrices),))],
        compiler_params=pltpu.CompilerParams(vmem_limit_bytes=40 * 1024 * 1024),
    )(rows, *factors, *matrices)


def body(out_grad, groups, picks, gates, w_gate, w_up, w_down, saved):
    group_count = lax.axis_size("group")
    member_count = lax.axis_size("member")
    experts = member_count // 2
    tok_count, width = out_grad.shape
    cap = 12 * tok_count // member_count
    slots = experts * cap
    same_core = [list(range(c, member_count, 2)) for c in range(2)]
    swap = [(i, i ^ 1) for i in range(member_count)]
    core = lax.axis_index("member") % 2
    group_shape = (group_count, width * SUB // LANES + 24, LANES)
    member_shape = (experts, width * WIDE // LANES + 48, LANES)

    def over_group(rows):
        return lax.all_to_all(rows, "group", split_axis=0, concat_axis=0, tiled=True)

    def over_member(rows):
        return lax.all_to_all(
            rows, "member", split_axis=0, concat_axis=0, axis_index_groups=same_core, tiled=True
        )

    def across(rows):
        return lax.ppermute(rows, "member", swap)

    w_gate, w_up, w_down, inputs = w_gate[0, 0], w_up[0, 0], w_down[0, 0], saved[0, 0]
    inputs = (inputs, w_gate, w_up, w_down)
    rows = (out_grad, groups.T, picks.T, gates.T)
    flags = jnp.stack([1 - core, core]).astype(jnp.int32)
    payload, *earlier = send(flags, rows, inputs, group_shape, cap)
    arrived = over_group(payload)
    prepared = prepare(jnp.stack([core, core]).astype(jnp.int32), inputs, tuple(earlier), cap)
    mine, yours, w_gate, w_up, w_down = prepared
    _, groups = lax.optimization_barrier((payload, groups.T))
    placing = call(
        place_kernel, [(group_count * SUB, tok_count), (group_count, tok_count)], groups
    )
    yours, w_down2, w_gate2, w_up2 = [across(x) for x in (yours, w_down, w_gate, w_up)]

    def route(rows):
        kernel = lambda *refs: route_kernel(*refs, width=width, cap=cap)
        return call(
            kernel, [member_shape, (slots, group_count * SUB), (slots, group_count)], rows
        )

    scaled, routing, routing9 = route(arrived)
    weights = (mine, yours, w_down, w_down2, w_gate, w_up, w_gate2, w_up2)
    scaled, placing, weights = lax.optimization_barrier((scaled, placing, weights))
    returned = over_member(expert_parts(over_member(scaled), *weights))
    sums = call(
        lambda *refs: gather_kernel(*refs, width=width),
        [group_shape],
        returned,
        routing,
        routing9,
    )
    return call(final_kernel, [(tok_count, width)], over_group(sums), *placing)


def solution(mesh):
    token = P(("dp", "group", "member"), None)
    weight = P("group", "member", None, None)
    return jax.shard_map(
        body,
        mesh=mesh,
        in_specs=(token,) * 4 + (weight,) * 3 + (P("group", "member", "dp", None),),
        out_specs=token,
        check_vma=False,
    )
```

```python
import jax
import jax.numpy as jnp
from jax import lax
from jax.experimental import pallas as pl
from jax.experimental.pallas import tpu as pltpu
from jax.sharding import PartitionSpec as P

LANES = 128
SUB = 8
WIDE = 16
F32 = jnp.float32
BF16 = jnp.bfloat16


def iota(shape, dim):
    return lax.broadcasted_iota(jnp.int32, shape, dim)


def dot(a, b, left=1, right=0):
    return lax.dot_general(
        a.astype(BF16), b.astype(BF16), (((left,), (right,)), ((), ())), preferred_element_type=F32
    )


def fold(rows):
    return rows.reshape(rows.shape[0], rows.shape[1] // LANES, LANES)


def unfold(rows):
    return rows.reshape(rows.shape[0], rows.shape[1] * LANES)


def pack_group(out_ref, main, ninth, extra):
    count, width = ninth.shape
    half = width // 2
    main = main.reshape(count, SUB, width)
    tiles = half // LANES
    for q in range(tiles):
        low = main[:, :, q * LANES : (q + 1) * LANES]
        high = main[:, :, half + q * LANES : half + (q + 1) * LANES]
        tile = jnp.concatenate([low, high], axis=1)
        out_ref[:, q * WIDE : (q + 1) * WIDE, :] = tile.astype(BF16)
    tail = out_ref.shape[1] - tiles * WIDE
    pad = tail - width // LANES - 1
    block = jnp.concatenate(
        [fold(ninth), extra.reshape(count, 1, LANES), jnp.zeros((count, pad, LANES), F32)], axis=1
    )
    out_ref[:, tiles * WIDE :, :] = block.astype(BF16)


def unpack_group(in_ref, width):
    count = in_ref.shape[0]
    tiles = width // 2 // LANES
    low, high = [], []
    for q in range(tiles):
        tile = in_ref[:, q * WIDE : (q + 1) * WIDE, :].astype(F32)
        low.append(tile[:, :SUB, :].reshape(count * SUB, LANES).astype(BF16))
        high.append(tile[:, SUB:, :].reshape(count * SUB, LANES).astype(BF16))
    main = jnp.concatenate(low + high, axis=1)
    block = in_ref[:, tiles * WIDE :, :].astype(F32)
    ninth = unfold(block[:, : width // LANES, :])
    extra = block[:, width // LANES, :]
    return main, ninth.astype(BF16), extra


def pack_member(out_ref, main, last):
    count = out_ref.shape[0]
    width = main.shape[1]
    tiles = width // LANES
    main = main.astype(BF16).reshape(count, WIDE, width)
    for q in range(tiles):
        out_ref[:, q * WIDE : (q + 1) * WIDE, :] = main[:, :, q * LANES : (q + 1) * LANES]
    room = (out_ref.shape[1] - tiles * WIDE) // 2
    pad = jnp.zeros((count, room - tiles, LANES), F32)
    last = fold(last)
    block = jnp.concatenate([last[:count], pad, last[count:], pad], axis=1)
    out_ref[:, tiles * WIDE :, :] = block.astype(BF16)


def unpack_member(in_ref, width):
    count = in_ref.shape[0]
    tiles = width // LANES
    main = [in_ref[:, q * WIDE : (q + 1) * WIDE, :].reshape(count * WIDE, LANES) for q in range(tiles)]
    main = jnp.concatenate(main, axis=1)
    room = (in_ref.shape[1] - tiles * WIDE) // 2
    block = in_ref[:, tiles * WIDE :, :].astype(F32)
    last = [unfold(block[:, s * room : s * room + tiles, :]) for s in range(2)]
    return main, jnp.concatenate(last, axis=0).astype(BF16)


def columns(rows):
    count = rows.shape[1]
    eye = (iota((count, count), 0) == iota((count, count), 1)).astype(F32)
    return dot(eye, rows.astype(F32), 1, 1)


def place(groups, tok_count, group_count):
    hit = groups[:, 0:1] == iota((tok_count, group_count), 1)
    for k in range(1, 3):
        hit = hit | (groups[:, k : k + 1] == iota((tok_count, group_count), 1))
    hit = hit.astype(F32)
    earlier = (iota((tok_count, tok_count), 1) < iota((tok_count, tok_count), 0)).astype(F32)
    position = jnp.where(hit > 0, dot(earlier, hit), 99.0)
    rows = group_count * SUB
    spread = (iota((rows, group_count), 0) >> 3 == iota((rows, group_count), 1)).astype(F32)
    at = dot(spread, position, 1, 1)
    main = (at == (iota((rows, tok_count), 0) & 7).astype(F32)).astype(F32)
    eye = (iota((group_count, group_count), 0) == iota((group_count, group_count), 1)).astype(F32)
    ninth = (dot(eye, position, 1, 1) == float(SUB)).astype(F32)
    return main, ninth, spread


def send_kernel(
    grad_hbm, groups_hbm, picks_hbm, gates_hbm, out_ref, grad_ref, groups_ref, picks_ref, gates_ref, sems,
    *, group_count,
):
    pairs = (
        (groups_hbm, groups_ref), (picks_hbm, picks_ref), (gates_hbm, gates_ref), (grad_hbm, grad_ref)
    )
    copies = [pltpu.make_async_copy(a, b, sems.at[i]) for i, (a, b) in enumerate(pairs)]
    for copy in copies:
        copy.start()
    for copy in copies[:3]:
        copy.wait()
    tok_count = grad_ref.shape[0]
    groups = columns(groups_ref[...]).astype(jnp.int32)
    picks = columns(picks_ref[...]).astype(jnp.int32)
    gates = columns(gates_ref[...])
    main, ninth, spread = place(groups, tok_count, group_count)
    table = jnp.zeros((tok_count, LANES), F32)
    for k in range(picks.shape[1]):
        pick = picks[:, k : k + 1]
        column = pick >> 3
        group = jnp.where(
            column == 0, groups[:, 0:1], jnp.where(column == 1, groups[:, 1:2], groups[:, 2:3])
        )
        expert = group * SUB + (pick & 7)
        table = table + jnp.where(expert == iota((tok_count, LANES), 1), gates[:, k : k + 1], 0.0)
    rows = group_count * SUB
    lane_of = iota((rows, LANES), 1)
    row_of = iota((rows, LANES), 0)
    same_within = ((iota((LANES, LANES), 0) & 7) == (iota((LANES, LANES), 1) & 7)).astype(F32)
    of_row = jnp.where(row_of >> 3 == lane_of >> 3, dot(main, table), 0.0)
    of_row = jnp.where((row_of & 7) == lane_of >> 3, dot(of_row, same_within), 0.0)
    extra = dot(spread, of_row, 0, 0)
    lane_of = iota((group_count, LANES), 1)
    of_row = jnp.where(iota((group_count, LANES), 0) == lane_of >> 3, dot(ninth, table), 0.0)
    extra = extra + jnp.where(lane_of >> 3 == SUB, dot(of_row, same_within), 0.0)
    copies[3].wait()
    grad = grad_ref[...]
    pack_group(out_ref, dot(main, grad), dot(ninth, grad), extra)


def route_kernel(in_ref, out_ref, main_ref, ninth_ref, *, width, cap):
    count, experts = in_ref.shape[0], SUB
    rows = count * SUB
    main, ninth, extra = unpack_group(in_ref, width)
    spread = (iota((count, rows), 1) >> 3 == iota((count, rows), 0)).astype(F32)
    wide = dot(extra, spread, 0, 0)
    wide = jnp.where(iota((LANES, rows), 0) >> 3 == (iota((LANES, rows), 1) & 7), wide, 0.0)
    pick = ((iota((experts, LANES), 1) & 7) == iota((experts, LANES), 0)).astype(F32)
    gate = dot(pick, wide)
    pick = (iota((experts, LANES), 1) == iota((experts, LANES), 0) + SUB * SUB).astype(F32)
    gate9 = dot(pick, extra, 1, 1)
    on, on9 = (gate > 0).astype(F32), (gate9 > 0).astype(F32)
    mm = (iota((rows, rows), 0) < iota((rows, rows), 1)).astype(F32)
    nm = (iota((count, rows), 0) < iota((count, rows), 1) >> 3).astype(F32)
    mn = (iota((rows, count), 0) >> 3 <= iota((rows, count), 1)).astype(F32)
    nn = (iota((count, count), 0) < iota((count, count), 1)).astype(F32)
    rank = dot(on, mm) + dot(on9, nm)
    rank9 = dot(on, mn) + dot(on9, nn)

    def weights(expert_of, slot_of):
        slots = expert_of.shape[0]
        expand = (expert_of[:, :experts] == iota((slots, experts), 1)).astype(F32)

        def one(rank, gate):
            slot = slot_of[:, : rank.shape[1]].astype(F32)
            value = dot(expand, gate)
            return jnp.where((dot(expand, rank) == slot) & (value > 0), value, 0.0)

        return one(rank, gate), one(rank9, gate9)

    big = iota((experts * WIDE, LANES), 0)
    small = iota((2 * experts, LANES), 0)
    weigh, weigh9 = weights(big >> 4, big & 15)
    last, last9 = weights(small & 7, WIDE + (small >> 3))
    first = dot(weigh, main) + dot(weigh9, ninth)
    second = dot(last, main) + dot(last9, ninth)
    pack_member(out_ref, first, second)
    main_ref[: experts * WIDE, :] = (weigh > 0).astype(F32).astype(BF16)
    main_ref[experts * WIDE :, :] = (last > 0).astype(F32).astype(BF16)
    ninth_ref[: experts * WIDE, :] = (weigh9 > 0).astype(F32).astype(BF16)
    ninth_ref[experts * WIDE :, :] = (last9 > 0).astype(F32).astype(BF16)


def prepare_kernel(flags_ref, *refs, cap):
    saved_hbm, gate_hbm, up_hbm, down_hbm = refs[:4]
    mine_hbm, yours_hbm, gate_t, up_t, down_t = refs[-12:-7]
    saved_ref, tall_ref, wide_ref, mine_ref, yours_ref, factor_sems, sems = refs[-7:]

    @pl.when(flags_ref[0] == 1)
    def _():
        def load(source, target):
            return pltpu.make_async_copy(source, target, sems.at[0])

        def store(source, target):
            return pltpu.make_async_copy(source, target, sems.at[1])

        first_load = pltpu.make_async_copy(saved_hbm, saved_ref, factor_sems.at[0])
        first_load.start()
        gate_load, up_load = load(gate_hbm, tall_ref), load(up_hbm, tall_ref)
        down_load = load(down_hbm, wide_ref)
        gate_load.start()
        slots = saved_ref.shape[0]
        half = slots // 2
        experts = half // cap
        core = flags_ref[1]
        row = iota((slots, slots), 0)
        column = jnp.where(row < half, core, 1 - core)
        row = jnp.where(row < half, row, row - half)
        late = row - experts * WIDE
        member = jnp.where(late < 0, row >> 4, late & 7)
        place_in = jnp.where(late < 0, row & 15, WIDE + (late >> 3))
        order = iota((slots, slots), 1) == (2 * member + column) * cap + place_in
        first_load.wait()
        rows = dot(order.astype(F32), saved_ref[...]).astype(BF16)
        gate_load.wait()
        pre_gate = dot(rows, tall_ref[...])
        wide_ref[...] = tall_ref[...].T
        gate_store = store(wide_ref, gate_t)
        gate_store.start()
        up_load.start()
        up_load.wait()
        pre_up = dot(rows, tall_ref[...])
        gate = 1.0 / (1.0 + jnp.exp(-pre_gate))
        first = pre_up * gate * (1.0 + pre_gate * (1.0 - gate))
        factors = jnp.concatenate([first, pre_gate * gate], axis=1)
        mine_ref[...] = factors[:half]
        yours_ref[...] = factors[half:]
        stores = [
            pltpu.make_async_copy(mine_ref, mine_hbm, factor_sems.at[1]),
            pltpu.make_async_copy(yours_ref, yours_hbm, factor_sems.at[2]),
        ]
        for one in stores:
            one.start()
        gate_store.wait()
        wide_ref[...] = tall_ref[...].T
        up_store = store(wide_ref, up_t)
        up_store.start()
        up_store.wait()
        down_load.start()
        down_load.wait()
        tall_ref[...] = wide_ref[...].T
        down_store = store(tall_ref, down_t)
        down_store.start()
        down_store.wait()
        for one in stores:
            one.wait()


def prepared_shapes(saved, gate, up, down):
    slots, hidden = saved.shape[0], gate.shape[1]
    factor = jax.ShapeDtypeStruct((slots // 2, 2 * hidden), F32)
    outs = [factor, factor] + [
        jax.ShapeDtypeStruct(weight.shape[::-1], BF16) for weight in (gate, up, down)
    ]
    scratch = [pltpu.VMEM(x.shape, x.dtype) for x in (saved, gate, down, factor, factor)]
    return [pltpu.HBM(x.shape, x.dtype) for x in outs], scratch + [
        pltpu.SemaphoreType.DMA((3,)),
        pltpu.SemaphoreType.DMA((2,)),
    ]


def send(flags, rows, inputs, group_shape, cap):
    outs, scratch = prepared_shapes(*inputs)

    def kernel(flags_ref, *refs):
        send_kernel(*refs[:4], refs[8], *refs[14:19], group_count=group_shape[0])
        prepare_kernel(flags_ref, *refs[4:8], *refs[9:14], *refs[19:], cap=cap)

    return pl.pallas_call(
        kernel,
        out_shape=[jax.ShapeDtypeStruct(group_shape, BF16)] + outs,
        in_specs=[pl.BlockSpec(memory_space=pltpu.SMEM)] + [HBM] * 8,
        out_specs=[VMEM] + [HBM] * len(outs),
        scratch_shapes=[pltpu.VMEM(x.shape, x.dtype) for x in rows]
        + [pltpu.SemaphoreType.DMA((4,))]
        + scratch,
        compiler_params=pltpu.CompilerParams(vmem_limit_bytes=40 * 1024 * 1024),
    )(flags, *in_hbm(rows), *in_hbm(inputs))


def prepare(flags, inputs, earlier, cap):
    outs, scratch = prepared_shapes(*inputs)
    return pl.pallas_call(
        lambda *refs: prepare_kernel(*refs, cap=cap),
        out_shape=outs,
        in_specs=[pl.BlockSpec(memory_space=pltpu.SMEM)] + [HBM] * (4 + len(earlier)),
        out_specs=[HBM] * len(outs),
        scratch_shapes=scratch,
        input_output_aliases={5 + i: i for i in range(len(earlier))},
        cost_estimate=pl.CostEstimate(flops=6 * 10**9, bytes_accessed=20 * 10**6, transcendentals=0),
        compiler_params=pltpu.CompilerParams(vmem_limit_bytes=40 * 1024 * 1024),
    )(flags, *in_hbm(inputs), *in_hbm(earlier))


def expert_kernel(
    in_ref, factor_ref, factor2_ref, down_hbm, down2_hbm, gate_hbm, up_hbm, gate2_hbm, up2_hbm, out_ref,
    down_ref, down2_ref, gate_ref, up_ref, gate2_ref, up2_ref, sems,
):
    width, hidden = down_ref.shape
    sources = (down_hbm, down2_hbm, gate_hbm, up_hbm, gate2_hbm, up2_hbm)
    weights = (down_ref, down2_ref, gate_ref, up_ref, gate2_ref, up2_ref)
    copies = [
        pltpu.make_async_copy(source, weight, sems.at[i])
        for i, (source, weight) in enumerate(zip(sources, weights))
    ]
    for copy in copies:
        copy.start()
    main, last = unpack_member(in_ref, width)
    split = main.shape[0]
    rows = jnp.concatenate([main, last], axis=0)
    sides = []
    for i, factor in enumerate((factor_ref, factor2_ref)):
        copies[i].wait()
        grad = dot(rows, weights[i][...])
        sides.append((grad * factor[:, :hidden]).astype(BF16))
        sides.append((grad * factor[:, hidden:]).astype(BF16))
    copies[2].wait()
    parts = dot(sides[0], gate_ref[...])
    for side, weight, copy in zip(sides[1:], (up_ref, gate2_ref, up2_ref), copies[3:]):
        copy.wait()
        parts = parts + dot(side, weight[...])
    pack_member(out_ref, parts[:split], parts[split:])


def gather_kernel(in_ref, main_ref, ninth_ref, out_ref, *, width):
    main, last = unpack_member(in_ref, width)
    split = main.shape[0]
    total = dot(main_ref[:split, :], main, 0, 0) + dot(main_ref[split:, :], last, 0, 0)
    total9 = dot(ninth_ref[:split, :], main, 0, 0) + dot(ninth_ref[split:, :], last, 0, 0)
    pack_group(out_ref, total, total9, jnp.zeros((out_ref.shape[0], LANES), F32))


def place_kernel(groups_ref, main_ref, ninth_ref):
    groups = columns(groups_ref[...]).astype(jnp.int32)
    main, ninth, _ = place(groups, main_ref.shape[1], ninth_ref.shape[0])
    main_ref[...] = main.astype(BF16)
    ninth_ref[...] = ninth.astype(BF16)


def final_kernel(in_ref, main_ref, ninth_ref, out_ref):
    rows, rows9, _ = unpack_group(in_ref, out_ref.shape[1])
    total = dot(main_ref[...], rows, 0, 0) + dot(ninth_ref[...], rows9, 0, 0)
    out_ref[...] = total.astype(BF16)


HBM = pl.BlockSpec(memory_space=pltpu.HBM)
VMEM = pl.BlockSpec(memory_space=pltpu.VMEM)


def in_hbm(arrays):
    return [pltpu.with_memory_space_constraint(x, pltpu.HBM) for x in arrays]


def call(kernel, outs, *args):
    shapes = [jax.ShapeDtypeStruct(shape, BF16) for shape in outs]
    return pl.pallas_call(
        kernel,
        out_shape=shapes if len(shapes) > 1 else shapes[0],
        compiler_params=pltpu.CompilerParams(vmem_limit_bytes=32 * 1024 * 1024),
    )(*args)


def expert_parts(rows, *weights):
    factors, matrices = weights[:2], in_hbm(weights[2:])
    return pl.pallas_call(
        expert_kernel,
        out_shape=jax.ShapeDtypeStruct(rows.shape, BF16),
        in_specs=[VMEM] * 3 + [HBM] * 6,
        out_specs=VMEM,
        scratch_shapes=[pltpu.VMEM(weight.shape, BF16) for weight in matrices]
        + [pltpu.SemaphoreType.DMA((len(matrices),))],
        compiler_params=pltpu.CompilerParams(vmem_limit_bytes=40 * 1024 * 1024),
    )(rows, *factors, *matrices)


def body(out_grad, groups, picks, gates, w_gate, w_up, w_down, saved):
    group_count = lax.axis_size("group")
    member_count = lax.axis_size("member")
    experts = member_count // 2
    tok_count, width = out_grad.shape
    cap = 12 * tok_count // member_count
    slots = experts * cap
    same_core = [list(range(c, member_count, 2)) for c in range(2)]
    swap = [(i, i ^ 1) for i in range(member_count)]
    core = lax.axis_index("member") % 2
    group_shape = (group_count, width * SUB // LANES + 24, LANES)
    member_shape = (experts, width * WIDE // LANES + 48, LANES)

    def over_group(rows):
        return lax.all_to_all(rows, "group", split_axis=0, concat_axis=0, tiled=True)

    def over_member(rows):
        return lax.all_to_all(
            rows, "member", split_axis=0, concat_axis=0, axis_index_groups=same_core, tiled=True
        )

    def across(rows):
        return lax.ppermute(rows, "member", swap)

    w_gate, w_up, w_down, inputs = w_gate[0, 0], w_up[0, 0], w_down[0, 0], saved[0, 0]
    inputs = (inputs, w_gate, w_up, w_down)
    rows = (out_grad, groups.T, picks.T, gates.T)
    flags = jnp.stack([1 - core, core]).astype(jnp.int32)
    payload, *earlier = send(flags, rows, inputs, group_shape, cap)
    arrived = over_group(payload)
    prepared = prepare(jnp.stack([core, core]).astype(jnp.int32), inputs, tuple(earlier), cap)
    mine, yours, w_gate, w_up, w_down = prepared
    yours, w_down2, w_gate2, w_up2 = [across(x) for x in (yours, w_down, w_gate, w_up)]

    def route(rows):
        kernel = lambda *refs: route_kernel(*refs, width=width, cap=cap)
        return call(
            kernel, [member_shape, (slots, group_count * SUB), (slots, group_count)], rows
        )

    scaled, routing, routing9 = route(arrived)
    weights = (mine, yours, w_down, w_down2, w_gate, w_up, w_gate2, w_up2)
    scaled, weights = lax.optimization_barrier((scaled, weights))
    returned = over_member(expert_parts(over_member(scaled), *weights))
    sums = call(
        lambda *refs: gather_kernel(*refs, width=width),
        [group_shape],
        returned,
        routing,
        routing9,
    )
    sums, groups = lax.optimization_barrier((sums, groups.T))
    back = over_group(sums)
    placing = call(
        place_kernel, [(group_count * SUB, tok_count), (group_count, tok_count)], groups
    )
    return call(final_kernel, [(tok_count, width)], back, *placing)


def solution(mesh):
    token = P(("dp", "group", "member"), None)
    weight = P("group", "member", None, None)
    return jax.shard_map(
        body,
        mesh=mesh,
        in_specs=(token,) * 4 + (weight,) * 3 + (P("group", "member", "dp", None),),
        out_specs=token,
        check_vma=False,
    )
```

```python
import jax
import jax.numpy as jnp
from jax import lax
from jax.experimental import pallas as pl
from jax.experimental.pallas import tpu as pltpu
from jax.sharding import PartitionSpec as P

LANES = 128
SUB = 8
WIDE = 16
F32 = jnp.float32
BF16 = jnp.bfloat16


def iota(shape, dim):
    return lax.broadcasted_iota(jnp.int32, shape, dim)


def dot(a, b, left=1, right=0):
    return lax.dot_general(
        a.astype(BF16), b.astype(BF16), (((left,), (right,)), ((), ())), preferred_element_type=F32
    )


def fold(rows):
    return rows.reshape(rows.shape[0], rows.shape[1] // LANES, LANES)


def unfold(rows):
    return rows.reshape(rows.shape[0], rows.shape[1] * LANES)


def pack_group(out_ref, main, ninth, extra):
    count, width = ninth.shape
    half = width // 2
    main = main.reshape(count, SUB, width)
    tiles = half // LANES
    for q in range(tiles):
        low = main[:, :, q * LANES : (q + 1) * LANES]
        high = main[:, :, half + q * LANES : half + (q + 1) * LANES]
        tile = jnp.concatenate([low, high], axis=1)
        out_ref[:, q * WIDE : (q + 1) * WIDE, :] = tile.astype(BF16)
    tail = out_ref.shape[1] - tiles * WIDE
    pad = tail - width // LANES - 1
    block = jnp.concatenate(
        [fold(ninth), extra.reshape(count, 1, LANES), jnp.zeros((count, pad, LANES), F32)], axis=1
    )
    out_ref[:, tiles * WIDE :, :] = block.astype(BF16)


def pack_halves(out_hbm, buffer, sems, main, ninth, extra):
    half = buffer.shape[0] // 2
    copies = []
    for i in range(2):
        part = slice(i * half, (i + 1) * half)
        at = pl.ds(i * half, half)
        rows = main[i * half * SUB : (i + 1) * half * SUB]
        pack_group(buffer.at[at], rows, ninth[part], extra[part])
        copies.append(pltpu.make_async_copy(buffer.at[at], out_hbm.at[at], sems.at[i]))
        copies[-1].start()
    for copy in copies:
        copy.wait()


def unpack_group(in_ref, width):
    count = in_ref.shape[0]
    tiles = width // 2 // LANES
    low, high = [], []
    for q in range(tiles):
        tile = in_ref[:, q * WIDE : (q + 1) * WIDE, :].astype(F32)
        low.append(tile[:, :SUB, :].reshape(count * SUB, LANES).astype(BF16))
        high.append(tile[:, SUB:, :].reshape(count * SUB, LANES).astype(BF16))
    main = jnp.concatenate(low + high, axis=1)
    block = in_ref[:, tiles * WIDE :, :].astype(F32)
    ninth = unfold(block[:, : width // LANES, :])
    extra = block[:, width // LANES, :]
    return main, ninth.astype(BF16), extra


def pack_member(out_ref, main, last):
    count = out_ref.shape[0]
    width = main.shape[1]
    tiles = width // LANES
    main = main.astype(BF16).reshape(count, WIDE, width)
    for q in range(tiles):
        out_ref[:, q * WIDE : (q + 1) * WIDE, :] = main[:, :, q * LANES : (q + 1) * LANES]
    room = (out_ref.shape[1] - tiles * WIDE) // 2
    pad = jnp.zeros((count, room - tiles, LANES), F32)
    last = fold(last)
    block = jnp.concatenate([last[:count], pad, last[count:], pad], axis=1)
    out_ref[:, tiles * WIDE :, :] = block.astype(BF16)


def unpack_member(in_ref, width):
    count = in_ref.shape[0]
    tiles = width // LANES
    main = [in_ref[:, q * WIDE : (q + 1) * WIDE, :].reshape(count * WIDE, LANES) for q in range(tiles)]
    main = jnp.concatenate(main, axis=1)
    room = (in_ref.shape[1] - tiles * WIDE) // 2
    block = in_ref[:, tiles * WIDE :, :].astype(F32)
    last = [unfold(block[:, s * room : s * room + tiles, :]) for s in range(2)]
    return main, jnp.concatenate(last, axis=0).astype(BF16)


def columns(rows):
    count = rows.shape[1]
    eye = (iota((count, count), 0) == iota((count, count), 1)).astype(F32)
    return dot(eye, rows.astype(F32), 1, 1)


def place(groups, tok_count, group_count):
    hit = groups[:, 0:1] == iota((tok_count, group_count), 1)
    for k in range(1, 3):
        hit = hit | (groups[:, k : k + 1] == iota((tok_count, group_count), 1))
    hit = hit.astype(F32)
    earlier = (iota((tok_count, tok_count), 1) < iota((tok_count, tok_count), 0)).astype(F32)
    position = jnp.where(hit > 0, dot(earlier, hit), 99.0)
    rows = group_count * SUB
    spread = (iota((rows, group_count), 0) >> 3 == iota((rows, group_count), 1)).astype(F32)
    at = dot(spread, position, 1, 1)
    main = (at == (iota((rows, tok_count), 0) & 7).astype(F32)).astype(F32)
    eye = (iota((group_count, group_count), 0) == iota((group_count, group_count), 1)).astype(F32)
    ninth = (dot(eye, position, 1, 1) == float(SUB)).astype(F32)
    return main, ninth, spread


def send_kernel(
    grad_hbm, groups_hbm, picks_hbm, gates_hbm, out_hbm, grad_ref, groups_ref, picks_ref, gates_ref, sems,
    buffer, out_sems, *, group_count,
):
    pairs = (
        (groups_hbm, groups_ref), (picks_hbm, picks_ref), (gates_hbm, gates_ref), (grad_hbm, grad_ref)
    )
    copies = [pltpu.make_async_copy(a, b, sems.at[i]) for i, (a, b) in enumerate(pairs)]
    for copy in copies:
        copy.start()
    for copy in copies[:3]:
        copy.wait()
    tok_count = grad_ref.shape[0]
    groups = columns(groups_ref[...]).astype(jnp.int32)
    picks = columns(picks_ref[...]).astype(jnp.int32)
    gates = columns(gates_ref[...])
    main, ninth, spread = place(groups, tok_count, group_count)
    table = jnp.zeros((tok_count, LANES), F32)
    for k in range(picks.shape[1]):
        pick = picks[:, k : k + 1]
        column = pick >> 3
        group = jnp.where(
            column == 0, groups[:, 0:1], jnp.where(column == 1, groups[:, 1:2], groups[:, 2:3])
        )
        expert = group * SUB + (pick & 7)
        table = table + jnp.where(expert == iota((tok_count, LANES), 1), gates[:, k : k + 1], 0.0)
    rows = group_count * SUB
    lane_of = iota((rows, LANES), 1)
    row_of = iota((rows, LANES), 0)
    same_within = ((iota((LANES, LANES), 0) & 7) == (iota((LANES, LANES), 1) & 7)).astype(F32)
    of_row = jnp.where(row_of >> 3 == lane_of >> 3, dot(main, table), 0.0)
    of_row = jnp.where((row_of & 7) == lane_of >> 3, dot(of_row, same_within), 0.0)
    extra = dot(spread, of_row, 0, 0)
    lane_of = iota((group_count, LANES), 1)
    of_row = jnp.where(iota((group_count, LANES), 0) == lane_of >> 3, dot(ninth, table), 0.0)
    extra = extra + jnp.where(lane_of >> 3 == SUB, dot(of_row, same_within), 0.0)
    copies[3].wait()
    grad = grad_ref[...]
    pack_halves(out_hbm, buffer, out_sems, dot(main, grad), dot(ninth, grad), extra)


def route_kernel(in_ref, out_ref, main_ref, ninth_ref, *, width, cap):
    count, experts = in_ref.shape[0], SUB
    rows = count * SUB
    main, ninth, extra = unpack_group(in_ref, width)
    spread = (iota((count, rows), 1) >> 3 == iota((count, rows), 0)).astype(F32)
    wide = dot(extra, spread, 0, 0)
    wide = jnp.where(iota((LANES, rows), 0) >> 3 == (iota((LANES, rows), 1) & 7), wide, 0.0)
    pick = ((iota((experts, LANES), 1) & 7) == iota((experts, LANES), 0)).astype(F32)
    gate = dot(pick, wide)
    pick = (iota((experts, LANES), 1) == iota((experts, LANES), 0) + SUB * SUB).astype(F32)
    gate9 = dot(pick, extra, 1, 1)
    on, on9 = (gate > 0).astype(F32), (gate9 > 0).astype(F32)
    mm = (iota((rows, rows), 0) < iota((rows, rows), 1)).astype(F32)
    nm = (iota((count, rows), 0) < iota((count, rows), 1) >> 3).astype(F32)
    mn = (iota((rows, count), 0) >> 3 <= iota((rows, count), 1)).astype(F32)
    nn = (iota((count, count), 0) < iota((count, count), 1)).astype(F32)
    rank = dot(on, mm) + dot(on9, nm)
    rank9 = dot(on, mn) + dot(on9, nn)

    def weights(expert_of, slot_of):
        slots = expert_of.shape[0]
        expand = (expert_of[:, :experts] == iota((slots, experts), 1)).astype(F32)

        def one(rank, gate):
            slot = slot_of[:, : rank.shape[1]].astype(F32)
            value = dot(expand, gate)
            return jnp.where((dot(expand, rank) == slot) & (value > 0), value, 0.0)

        return one(rank, gate), one(rank9, gate9)

    big = iota((experts * WIDE, LANES), 0)
    small = iota((2 * experts, LANES), 0)
    weigh, weigh9 = weights(big >> 4, big & 15)
    last, last9 = weights(small & 7, WIDE + (small >> 3))
    first = dot(weigh, main) + dot(weigh9, ninth)
    second = dot(last, main) + dot(last9, ninth)
    pack_member(out_ref, first, second)
    main_ref[: experts * WIDE, :] = (weigh > 0).astype(F32).astype(BF16)
    main_ref[experts * WIDE :, :] = (last > 0).astype(F32).astype(BF16)
    ninth_ref[: experts * WIDE, :] = (weigh9 > 0).astype(F32).astype(BF16)
    ninth_ref[experts * WIDE :, :] = (last9 > 0).astype(F32).astype(BF16)


def prepare_kernel(flags_ref, *refs, cap):
    saved_hbm, gate_hbm, up_hbm, down_hbm = refs[:4]
    mine_hbm, yours_hbm, gate_t, up_t, down_t = refs[-12:-7]
    saved_ref, tall_ref, wide_ref, mine_ref, yours_ref, factor_sems, sems = refs[-7:]

    @pl.when(flags_ref[0] == 1)
    def _():
        def load(source, target):
            return pltpu.make_async_copy(source, target, sems.at[0])

        def store(source, target):
            return pltpu.make_async_copy(source, target, sems.at[1])

        first_load = pltpu.make_async_copy(saved_hbm, saved_ref, factor_sems.at[0])
        first_load.start()
        gate_load, up_load = load(gate_hbm, tall_ref), load(up_hbm, tall_ref)
        down_load = load(down_hbm, wide_ref)
        gate_load.start()
        slots = saved_ref.shape[0]
        half = slots // 2
        experts = half // cap
        core = flags_ref[1]
        row = iota((slots, slots), 0)
        column = jnp.where(row < half, core, 1 - core)
        row = jnp.where(row < half, row, row - half)
        late = row - experts * WIDE
        member = jnp.where(late < 0, row >> 4, late & 7)
        place_in = jnp.where(late < 0, row & 15, WIDE + (late >> 3))
        order = iota((slots, slots), 1) == (2 * member + column) * cap + place_in
        first_load.wait()
        rows = dot(order.astype(F32), saved_ref[...]).astype(BF16)
        gate_load.wait()
        pre_gate = dot(rows, tall_ref[...])
        wide_ref[...] = tall_ref[...].T
        gate_store = store(wide_ref, gate_t)
        gate_store.start()
        up_load.start()
        up_load.wait()
        pre_up = dot(rows, tall_ref[...])
        gate = 1.0 / (1.0 + jnp.exp(-pre_gate))
        first = pre_up * gate * (1.0 + pre_gate * (1.0 - gate))
        factors = jnp.concatenate([first, pre_gate * gate], axis=1)
        mine_ref[...] = factors[:half]
        yours_ref[...] = factors[half:]
        stores = [
            pltpu.make_async_copy(mine_ref, mine_hbm, factor_sems.at[1]),
            pltpu.make_async_copy(yours_ref, yours_hbm, factor_sems.at[2]),
        ]
        for one in stores:
            one.start()
        gate_store.wait()
        wide_ref[...] = tall_ref[...].T
        up_store = store(wide_ref, up_t)
        up_store.start()
        up_store.wait()
        down_load.start()
        down_load.wait()
        tall_ref[...] = wide_ref[...].T
        down_store = store(tall_ref, down_t)
        down_store.start()
        down_store.wait()
        for one in stores:
            one.wait()


def prepared_shapes(saved, gate, up, down):
    slots, hidden = saved.shape[0], gate.shape[1]
    factor = jax.ShapeDtypeStruct((slots // 2, 2 * hidden), F32)
    outs = [factor, factor] + [
        jax.ShapeDtypeStruct(weight.shape[::-1], BF16) for weight in (gate, up, down)
    ]
    scratch = [pltpu.VMEM(x.shape, x.dtype) for x in (saved, gate, down, factor, factor)]
    return [pltpu.HBM(x.shape, x.dtype) for x in outs], scratch + [
        pltpu.SemaphoreType.DMA((3,)),
        pltpu.SemaphoreType.DMA((2,)),
    ]


def send(flags, rows, inputs, group_shape, cap):
    outs, scratch = prepared_shapes(*inputs)

    def kernel(flags_ref, *refs):
        send_kernel(*refs[:4], refs[8], *refs[14:21], group_count=group_shape[0])
        prepare_kernel(flags_ref, *refs[4:8], *refs[9:14], *refs[21:], cap=cap)

    return pl.pallas_call(
        kernel,
        out_shape=[pltpu.HBM(group_shape, BF16)] + outs,
        in_specs=[pl.BlockSpec(memory_space=pltpu.SMEM)] + [HBM] * 8,
        out_specs=[HBM] * (1 + len(outs)),
        scratch_shapes=[pltpu.VMEM(x.shape, x.dtype) for x in rows]
        + [pltpu.SemaphoreType.DMA((4,)), pltpu.VMEM(group_shape, BF16), pltpu.SemaphoreType.DMA((2,))]
        + scratch,
        compiler_params=pltpu.CompilerParams(vmem_limit_bytes=40 * 1024 * 1024),
    )(flags, *in_hbm(rows), *in_hbm(inputs))


def prepare(flags, inputs, earlier, cap):
    outs, scratch = prepared_shapes(*inputs)
    return pl.pallas_call(
        lambda *refs: prepare_kernel(*refs, cap=cap),
        out_shape=outs,
        in_specs=[pl.BlockSpec(memory_space=pltpu.SMEM)] + [HBM] * (4 + len(earlier)),
        out_specs=[HBM] * len(outs),
        scratch_shapes=scratch,
        input_output_aliases={5 + i: i for i in range(len(earlier))},
        cost_estimate=pl.CostEstimate(flops=6 * 10**9, bytes_accessed=20 * 10**6, transcendentals=0),
        compiler_params=pltpu.CompilerParams(vmem_limit_bytes=40 * 1024 * 1024),
    )(flags, *in_hbm(inputs), *in_hbm(earlier))


def expert_kernel(
    in_ref, factor_ref, factor2_ref, down_hbm, down2_hbm, gate_hbm, up_hbm, gate2_hbm, up2_hbm, out_ref,
    down_ref, down2_ref, gate_ref, up_ref, gate2_ref, up2_ref, sems,
):
    width, hidden = down_ref.shape
    sources = (down_hbm, down2_hbm, gate_hbm, up_hbm, gate2_hbm, up2_hbm)
    weights = (down_ref, down2_ref, gate_ref, up_ref, gate2_ref, up2_ref)
    copies = [
        pltpu.make_async_copy(source, weight, sems.at[i])
        for i, (source, weight) in enumerate(zip(sources, weights))
    ]
    for copy in copies:
        copy.start()
    main, last = unpack_member(in_ref, width)
    split = main.shape[0]
    rows = jnp.concatenate([main, last], axis=0)
    sides = []
    for i, factor in enumerate((factor_ref, factor2_ref)):
        copies[i].wait()
        grad = dot(rows, weights[i][...])
        sides.append((grad * factor[:, :hidden]).astype(BF16))
        sides.append((grad * factor[:, hidden:]).astype(BF16))
    copies[2].wait()
    parts = dot(sides[0], gate_ref[...])
    for side, weight, copy in zip(sides[1:], (up_ref, gate2_ref, up2_ref), copies[3:]):
        copy.wait()
        parts = parts + dot(side, weight[...])
    pack_member(out_ref, parts[:split], parts[split:])


def gather_kernel(in_ref, main_ref, ninth_ref, out_hbm, buffer, sems, *, width):
    main, last = unpack_member(in_ref, width)
    split = main.shape[0]
    total = dot(main_ref[:split, :], main, 0, 0) + dot(main_ref[split:, :], last, 0, 0)
    total9 = dot(ninth_ref[:split, :], main, 0, 0) + dot(ninth_ref[split:, :], last, 0, 0)
    extra = jnp.zeros((buffer.shape[0], LANES), F32)
    pack_halves(out_hbm, buffer, sems, total, total9, extra)


def place_kernel(groups_ref, main_ref, ninth_ref):
    groups = columns(groups_ref[...]).astype(jnp.int32)
    main, ninth, _ = place(groups, main_ref.shape[1], ninth_ref.shape[0])
    main_ref[...] = main.astype(BF16)
    ninth_ref[...] = ninth.astype(BF16)


def final_kernel(in_ref, main_ref, ninth_ref, out_ref):
    rows, rows9, _ = unpack_group(in_ref, out_ref.shape[1])
    total = dot(main_ref[...], rows, 0, 0) + dot(ninth_ref[...], rows9, 0, 0)
    out_ref[...] = total.astype(BF16)


HBM = pl.BlockSpec(memory_space=pltpu.HBM)
VMEM = pl.BlockSpec(memory_space=pltpu.VMEM)


def in_hbm(arrays):
    return [pltpu.with_memory_space_constraint(x, pltpu.HBM) for x in arrays]


def call(kernel, outs, *args):
    shapes = [jax.ShapeDtypeStruct(shape, BF16) for shape in outs]
    return pl.pallas_call(
        kernel,
        out_shape=shapes if len(shapes) > 1 else shapes[0],
        compiler_params=pltpu.CompilerParams(vmem_limit_bytes=32 * 1024 * 1024),
    )(*args)


def expert_parts(rows, *weights):
    factors, matrices = weights[:2], in_hbm(weights[2:])
    return pl.pallas_call(
        expert_kernel,
        out_shape=jax.ShapeDtypeStruct(rows.shape, BF16),
        in_specs=[VMEM] * 3 + [HBM] * 6,
        out_specs=VMEM,
        scratch_shapes=[pltpu.VMEM(weight.shape, BF16) for weight in matrices]
        + [pltpu.SemaphoreType.DMA((len(matrices),))],
        compiler_params=pltpu.CompilerParams(vmem_limit_bytes=40 * 1024 * 1024),
    )(rows, *factors, *matrices)


def body(out_grad, groups, picks, gates, w_gate, w_up, w_down, saved):
    group_count = lax.axis_size("group")
    member_count = lax.axis_size("member")
    experts = member_count // 2
    tok_count, width = out_grad.shape
    cap = 12 * tok_count // member_count
    slots = experts * cap
    same_core = [list(range(c, member_count, 2)) for c in range(2)]
    swap = [(i, i ^ 1) for i in range(member_count)]
    core = lax.axis_index("member") % 2
    group_shape = (group_count, width * SUB // LANES + 24, LANES)
    member_shape = (experts, width * WIDE // LANES + 48, LANES)

    def over_group(rows):
        return lax.all_to_all(rows, "group", split_axis=0, concat_axis=0, tiled=True)

    def over_member(rows):
        return lax.all_to_all(
            rows, "member", split_axis=0, concat_axis=0, axis_index_groups=same_core, tiled=True
        )

    def across(rows):
        return lax.ppermute(rows, "member", swap)

    w_gate, w_up, w_down, inputs = w_gate[0, 0], w_up[0, 0], w_down[0, 0], saved[0, 0]
    inputs = (inputs, w_gate, w_up, w_down)
    rows = (out_grad, groups.T, picks.T, gates.T)
    flags = jnp.stack([1 - core, core]).astype(jnp.int32)
    payload, *earlier = send(flags, rows, inputs, group_shape, cap)
    arrived = over_group(payload)
    prepared = prepare(jnp.stack([core, core]).astype(jnp.int32), inputs, tuple(earlier), cap)
    mine, yours, w_gate, w_up, w_down = prepared
    yours, w_down2, w_gate2, w_up2 = [across(x) for x in (yours, w_down, w_gate, w_up)]

    def route(rows):
        kernel = lambda *refs: route_kernel(*refs, width=width, cap=cap)
        return call(
            kernel, [member_shape, (slots, group_count * SUB), (slots, group_count)], rows
        )

    scaled, routing, routing9 = route(arrived)
    weights = (mine, yours, w_down, w_down2, w_gate, w_up, w_gate2, w_up2)
    scaled, weights = lax.optimization_barrier((scaled, weights))
    returned = over_member(expert_parts(over_member(scaled), *weights))
    sums = pl.pallas_call(
        lambda *refs: gather_kernel(*refs, width=width),
        out_shape=pltpu.HBM(group_shape, BF16),
        in_specs=[VMEM] * 3,
        out_specs=HBM,
        scratch_shapes=[pltpu.VMEM(group_shape, BF16), pltpu.SemaphoreType.DMA((2,))],
        compiler_params=pltpu.CompilerParams(vmem_limit_bytes=32 * 1024 * 1024),
    )(returned, routing, routing9)
    sums, groups = lax.optimization_barrier((sums, groups.T))
    back = over_group(sums)
    placing = call(
        place_kernel, [(group_count * SUB, tok_count), (group_count, tok_count)], groups
    )
    return call(final_kernel, [(tok_count, width)], back, *placing)


def solution(mesh):
    token = P(("dp", "group", "member"), None)
    weight = P("group", "member", None, None)
    return jax.shard_map(
        body,
        mesh=mesh,
        in_specs=(token,) * 4 + (weight,) * 3 + (P("group", "member", "dp", None),),
        out_specs=token,
        check_vma=False,
    )
```
